512 devices in a mesh: section: 32 (over z, core), tp: 16 (over y, x).
Axes of the slice: x: 4, y: 4, z: 16, core: 2. Of those that a mesh axis runs over, the one named last changes fastest.
Arguments:
- patches: bfloat16 [4, 64, 3200], P(None, None, 'tp'), may hold values from -6 to 6
- w_in: bfloat16 [32, 3200, 3200], P('section', 'tp'), may hold values from -0.109375 to 0.109375
- w_out: bfloat16 [32, 3200, 3200], P('section', 'tp'), may hold values from -0.078125 to 0.078125
- w_proj: bfloat16 [3200, 8192], P('tp', 'section'), may hold values from -0.109375 to 0.109375
Outputs:
- image_embeds: bfloat16 [256, 8192], P('tp', 'section')
The draws below stay inside these ranges and needn't reach their ends.
All inputs are finite; a program needn't handle non-finite values.
Results may differ from the reference program's by a relative error of at most 0.035.
Values may be sent and summed in bfloat16 or wider, within the bound.
No kernel may reach another device: no remote copies, remote signals or barrier semaphores. Data moves between devices by JAX's collectives and lax.ppermute only.
A program may use at most 64 MiB of HBM per device.

```python
import jax
import jax.numpy as jnp
from jax import lax

VD = 3200
HID = 6400
LD = 8192
ROWS = 64
MICRO = 4
LAYERS = 16
HALF = 3200


def level_of(key, shape, split, smallest, high):
    gain = 1.0
    for axis_at, shards_of in split:
        draws = jax.random.uniform(jax.random.fold_in(jax.random.fold_in(key, 6), axis_at), (shards_of,), jnp.float32, smallest / len(split), high / len(split))
        gain = gain * jnp.repeat(jnp.exp(draws), shape[axis_at] // shards_of).reshape((-1,) + (1,) * (len(shape) - 1 - axis_at))
    return gain


def gaussian(key, dims, scale, bound, split=(), kind=jnp.bfloat16):
    result = scale * jax.random.normal(key, dims, jnp.float32)
    if split:
        result = result * level_of(key, dims, split, -0.22, 0.18)
    return jnp.clip(result, -bound, bound).astype(kind)


def setup_inputs(seed: int = 0) -> dict:
    key_of = jax.random.split(jax.random.key(seed), 5)
    return {
        "patches": gaussian(key_of[0], (MICRO, ROWS, VD), 1.0, 6.0, ((2, 16),)),
        "w_in": gaussian(key_of[1], (2 * LAYERS, HALF, VD), VD ** -0.5, 0.109375, ((0, 32), (1, 16))),
        "w_out": gaussian(key_of[2], (2 * LAYERS, VD, HALF), HID ** -0.5, 0.078125, ((0, 32), (1, 16))),
        "w_proj": gaussian(key_of[3], (VD, LD), VD ** -0.5, 0.109375, ((0, 16), (1, 32))),
    }


def reference(patches, w_in, w_out, w_proj):
    rows = patches.reshape(MICRO * ROWS, VD)
    for layer in range(LAYERS):
        values = rows.astype(jnp.float32)
        scale = jax.lax.rsqrt(lax.optimization_barrier(jnp.mean(values * values, axis=1, keepdims=True)) + 1e-06)
        normed = (values * scale).astype(jnp.bfloat16)
        branch = jnp.zeros((MICRO * ROWS, VD), jnp.float32)
        for half_index in range(2):
            which = 2 * layer + half_index
            hidden = jax.nn.gelu(jnp.dot(normed, w_in[which].T, preferred_element_type=jnp.float32)).astype(jnp.bfloat16)
            branch = branch + jnp.dot(hidden, w_out[which].T, preferred_element_type=jnp.float32)
        rows = (values + branch).astype(jnp.bfloat16)
    return jnp.dot(rows, w_proj, preferred_element_type=jnp.float32).astype(jnp.bfloat16)
```

```python
import functools

import jax
import jax.numpy as jnp
from jax import lax
from jax.experimental import pallas as pl
from jax.experimental.pallas import tpu as pltpu
from jax.sharding import Mesh, PartitionSpec as P

TILE = 640


def half_layer(first_ref, pair_ref, up_ref, down_ref, out_ref, hidden_ref):
    rows = pair_ref[0].astype(jnp.float32) + pair_ref[1].astype(jnp.float32)
    scale = lax.rsqrt(jnp.mean(rows * rows, axis=1, keepdims=True) + 1e-06)
    normed = (rows * scale).astype(jnp.bfloat16)
    units, width = up_ref.shape
    for start in range(0, units, TILE):
        part = lax.dot_general(
            normed,
            up_ref[start : start + TILE, :],
            (((1,), (1,)), ((), ())),
            preferred_element_type=jnp.float32,
        )
        hidden_ref[:, start : start + TILE] = jax.nn.gelu(part).astype(jnp.bfloat16)
    hidden = hidden_ref[...]
    keep = first_ref[0] == 1
    for start in range(0, width, TILE):
        part = lax.dot_general(
            hidden,
            down_ref[start : start + TILE, :],
            (((1,), (1,)), ((), ())),
            preferred_element_type=jnp.float32,
        )
        base = jnp.where(keep, rows[:, start : start + TILE], 0.0)
        out_ref[:, start : start + TILE] = (base + part).astype(jnp.bfloat16)


def apply_half(first, pair, up, down):
    _, row_count, width = pair.shape
    units = up.shape[0]
    return pl.pallas_call(
        half_layer,
        out_shape=jax.ShapeDtypeStruct((row_count, width), jnp.bfloat16),
        in_specs=[
            pl.BlockSpec(memory_space=pltpu.SMEM),
            pl.BlockSpec(memory_space=pltpu.VMEM),
            pl.BlockSpec(memory_space=pltpu.VMEM),
            pl.BlockSpec(memory_space=pltpu.VMEM),
        ],
        out_specs=pl.BlockSpec(memory_space=pltpu.VMEM),
        scratch_shapes=[pltpu.VMEM((row_count, units), jnp.bfloat16)],
        compiler_params=pltpu.CompilerParams(vmem_limit_bytes=10 * 2**20),
        cost_estimate=pl.CostEstimate(
            flops=4 * row_count * units * width,
            bytes_accessed=4 * units * width,
            transcendentals=row_count * units,
        ),
    )(first, pair, up, down)


def on_device(layers, patches, w_in, w_out, w_proj):
    plane = lax.axis_index("z")
    core = lax.axis_index("c")
    tp = ("y", "x")
    first = (core == 0).astype(jnp.int32).reshape(1)

    up = lax.all_gather(w_in[0], tp, axis=0, tiled=True)
    down = lax.all_gather(w_out[0], tp, axis=0, tiled=True)
    columns = lax.all_gather(w_proj, tp, axis=0, tiled=True)
    up = pltpu.with_memory_space_constraint(up, pltpu.VMEM)
    down = pltpu.with_memory_space_constraint(down, pltpu.VMEM)

    flat = patches.reshape(-1, patches.shape[2])
    mine = lax.all_to_all(flat, tp, split_axis=0, concat_axis=1, tiled=True)
    pair = jnp.stack([mine, jnp.zeros_like(mine)])
    for layer in range(layers):
        part = apply_half(first, pair, up, down)
        if layer < layers - 1:
            part = lax.ppermute(part, "z", [(layer, layer + 1)])
        pair = lax.all_gather(part, "c", axis=0, tiled=False)

    total = pair[0].astype(jnp.float32) + pair[1].astype(jnp.float32)
    rows = jnp.where(plane == layers - 1, total, 0.0).astype(jnp.bfloat16)
    holders = [layers - 1]
    step = layers // 2
    while step:
        route = [(held, (held + step) % layers) for held in holders]
        rows = rows + lax.ppermute(rows, "z", route)
        holders += [target for _, target in route]
        step //= 2
    return jnp.dot(rows, columns, preferred_element_type=jnp.float32).astype(jnp.bfloat16)


def solution(mesh):
    sections = mesh.shape["section"]
    grid = Mesh(mesh.devices.reshape(sections // 2, 2, 4, 4), ("z", "c", "y", "x"))
    section, tp = ("z", "c"), ("y", "x")
    return jax.shard_map(
        functools.partial(on_device, sections // 2),
        mesh=grid,
        in_specs=(
            P(None, None, tp),
            P(section, tp, None),
            P(section, tp, None),
            P(tp, section),
        ),
        out_specs=P(tp, section),
        check_vma=False,
    )
```

```python
import functools

import jax
import jax.numpy as jnp
from jax import lax
from jax.experimental import pallas as pl
from jax.experimental.pallas import tpu as pltpu
from jax.sharding import Mesh, PartitionSpec as P

SIDE = 4
OFFSETS = (0, 3, 1, 2)


def moved(block, axis, by):
    route = [(i, (i + by) % SIDE) for i in range(SIDE)]
    return lax.ppermute(block, axis, route)


def ring(top, bottom, axis):
    below_top = moved(top, axis, 1)
    above_bottom = moved(bottom, axis, -1)
    below_bottom = moved(bottom, axis, 1)
    above_top = moved(top, axis, -1)
    far_top = moved(below_top, axis, 1)
    far_bottom = moved(above_bottom, axis, -1)
    return (
        (top, below_top, above_top, far_top),
        (bottom, below_bottom, above_bottom, far_bottom),
    )


def in_order(parts, axis):
    place = lax.axis_index(axis)
    rows, width = parts[0].shape
    whole = jnp.zeros((SIDE, rows, width), parts[0].dtype)
    for part, offset in zip(parts, OFFSETS):
        at = lax.rem(place + offset, SIDE)
        whole = lax.dynamic_update_slice(whole, part[None], (at, 0, 0))
    return whole.reshape(SIDE * rows, width)


def product(left, right):
    return lax.dot_general(
        left, right, (((1,), (1,)), ((), ())), preferred_element_type=jnp.float32
    )


def half_layer(state_ref, pair_ref, *refs):
    sources, (out_ref, tops_ref, bottoms_ref, hidden_top, hidden_bottom, sems) = (
        refs[:16],
        refs[16:],
    )
    row_count, width = out_ref.shape
    high = tops_ref.shape[1] // SIDE
    low = bottoms_ref.shape[1] // SIDE
    block = high + low

    @pl.when(state_ref[0] == 0)
    def _():
        out_ref[...] = jnp.zeros_like(out_ref)

    @pl.when(state_ref[0] == 1)
    def _():
        copies = []
        for which in range(2):
            for index in range(1, SIDE):
                slot = 3 * which + index - 1
                for half, target in enumerate((tops_ref, bottoms_ref)):
                    copies.append(
                        pltpu.make_async_copy(
                            sources[8 * which + 4 * half + index],
                            target.at[slot],
                            sems.at[2 * slot + half],
                        )
                    )
        for copy in copies:
            copy.start()

        rows = pair_ref[0].astype(jnp.float32) + pair_ref[1].astype(jnp.float32)
        scale = lax.rsqrt(jnp.mean(rows * rows, axis=1, keepdims=True) + 1e-06)
        normed = (rows * scale).astype(jnp.bfloat16)

        def joined():
            tops = [hidden_top[i] for i in range(SIDE)]
            bottoms = [hidden_bottom[i] for i in range(SIDE)]
            return tops, bottoms

        def stage(which, left, finish):
            for index, offset in enumerate(OFFSETS):
                at = lax.rem(state_ref[2 + which] + offset, SIDE)
                for half, (target, store) in enumerate(
                    ((tops_ref, hidden_top), (bottoms_ref, hidden_bottom))
                ):
                    if index == 0:
                        right = sources[8 * which + 4 * half][...]
                    else:
                        slot = 3 * which + index - 1
                        copies[2 * slot + half].wait()
                        right = target[slot]
                    store[at] = finish(product(left, right))

        stage(0, normed, jax.nn.gelu)
        tops, bottoms = joined()
        pieces = []
        for y in range(SIDE):
            for x in range(SIDE):
                pieces.append(tops[y][:, x * high : (x + 1) * high])
                pieces.append(bottoms[y][:, x * low : (x + 1) * low])
        hidden = jnp.concatenate(pieces, axis=1).astype(jnp.bfloat16)
        stage(1, hidden, lambda part: part)
        tops, bottoms = joined()
        pieces = []
        for y in range(SIDE):
            for x in range(SIDE):
                pieces.append(tops[x][:, y * high : (y + 1) * high])
                pieces.append(bottoms[x][:, y * low : (y + 1) * low])
        total = jnp.concatenate(pieces, axis=1)
        base = jnp.where(state_ref[1] == 1, rows, 0.0)
        out_ref[...] = (base + total).astype(jnp.bfloat16)


def apply_half(state, pair, up, down):
    _, row_count, width = pair.shape
    (up_tops, up_bottoms), (down_tops, down_bottoms) = up, down
    sources = (*up_tops, *up_bottoms, *down_tops, *down_bottoms)
    own = (0, 4, 8, 12)
    sources = [
        pltpu.with_memory_space_constraint(s, pltpu.VMEM) if i in own else s
        for i, s in enumerate(sources)
    ]
    resident = pl.BlockSpec(memory_space=pltpu.VMEM)
    anywhere = pl.BlockSpec(memory_space=pl.ANY)
    high, low = up_tops[0].shape[0], up_bottoms[0].shape[0]
    return pl.pallas_call(
        half_layer,
        out_shape=jax.ShapeDtypeStruct((row_count, width), jnp.bfloat16),
        in_specs=[pl.BlockSpec(memory_space=pltpu.SMEM), resident]
        + [resident if i in own else anywhere for i in range(16)],
        out_specs=resident,
        scratch_shapes=[
            pltpu.VMEM((6, high, width), jnp.bfloat16),
            pltpu.VMEM((6, low, width), jnp.bfloat16),
            pltpu.VMEM((SIDE, row_count, high), jnp.float32),
            pltpu.VMEM((SIDE, row_count, low), jnp.float32),
            pltpu.SemaphoreType.DMA((12,)),
        ],
        compiler_params=pltpu.CompilerParams(vmem_limit_bytes=40 * 2**20),
        cost_estimate=pl.CostEstimate(
            flops=4 * row_count * width * width,
            bytes_accessed=3 * width * width,
            transcendentals=row_count * width,
        ),
        name="half_layer",
    )(state, pair, *sources)


def on_device(layers, patches, w_in, w_out, w_proj):
    plane = lax.axis_index("z")
    core = lax.axis_index("c")
    tp = ("y", "x")
    cut = w_in.shape[1] // 16 * 8 + 8

    flat = patches.reshape(-1, patches.shape[2])
    mine = lax.all_to_all(flat, tp, split_axis=0, concat_axis=1, tiled=True)
    pair = jnp.stack([mine, jnp.zeros_like(mine)])

    up_tops, up_bottoms = ring(w_in[0, :cut], w_in[0, cut:], "x")
    down_tops, down_bottoms = ring(w_out[0, :cut], w_out[0, cut:], "y")
    up_top, up_bottom = in_order(up_tops, "x"), in_order(up_bottoms, "x")
    down_top, down_bottom = in_order(down_tops, "y"), in_order(down_bottoms, "y")
    up_top, pair = lax.optimization_barrier((up_top, pair))
    up = ring(up_top, up_bottom, "y")
    down = ring(down_top, down_bottom, "x")
    columns = lax.all_gather(w_proj, tp, axis=0, tiled=True)

    places = [core == 0, lax.axis_index("y"), lax.axis_index("x")]
    for layer in range(layers):
        state = jnp.stack([plane == layer] + places).astype(jnp.int32)
        part = apply_half(state, pair, up, down)
        if layer < layers - 1:
            part = lax.ppermute(part, "z", [(layer, layer + 1)])
        pair = lax.all_gather(part, "c", axis=0, tiled=False)

    total = pair[0].astype(jnp.float32) + pair[1].astype(jnp.float32)
    rows = jnp.where(plane == layers - 1, total, 0.0).astype(jnp.bfloat16)
    holders = [layers - 1]
    step = layers // 2
    while step:
        route = [(held, (held + step) % layers) for held in holders]
        rows = rows + lax.ppermute(rows, "z", route)
        holders += [target for _, target in route]
        step //= 2
    return jnp.dot(rows, columns, preferred_element_type=jnp.float32).astype(jnp.bfloat16)


def solution(mesh):
    sections = mesh.shape["section"]
    grid = Mesh(
        mesh.devices.reshape(sections // 2, 2, SIDE, SIDE), ("z", "c", "y", "x")
    )
    section, tp = ("z", "c"), ("y", "x")
    return jax.shard_map(
        functools.partial(on_device, sections // 2),
        mesh=grid,
        in_specs=(
            P(None, None, tp),
            P(section, tp, None),
            P(section, tp, None),
            P(tp, section),
        ),
        out_specs=P(tp, section),
        check_vma=False,
    )
```

```python
import functools

import jax
import jax.numpy as jnp
from jax import lax
from jax.experimental import pallas as pl
from jax.experimental.pallas import tpu as pltpu
from jax.sharding import Mesh, PartitionSpec as P

SIDE = 4
OFFSETS = (0, 3, 1, 2)
INTRA = [(0, 1), (1, 0), (2, 3), (3, 2)]
INTER = [(0, 3), (3, 0), (1, 2), (2, 1)]


def moved(block, axis, by):
    route = [(i, (i + by) % SIDE) for i in range(SIDE)]
    return lax.ppermute(block, axis, route)


def ring(block, axis, halves):
    below = moved(block, axis, 1)
    above = moved(block, axis, -1)
    head = moved(halves(below)[0], axis, 1)
    tail = moved(halves(above)[1], axis, -1)
    return below, above, head, tail


def in_order(parts, place):
    rows, width = parts[0].shape
    whole = jnp.zeros((SIDE, rows, width), parts[0].dtype)
    for part, offset in zip(parts, OFFSETS):
        at = lax.rem(place + offset, SIDE)
        whole = lax.dynamic_update_slice(whole, part[None], (at, 0, 0))
    return whole.reshape(SIDE * rows, width)


def product(left, right):
    return lax.dot_general(
        left, right, (((1,), (1,)), ((), ())), preferred_element_type=jnp.float32
    )


def quarter_layer(state_ref, pair_ref, *refs):
    up_refs, down_refs = refs[:5], refs[5:9]
    out_ref, near_ref, far_ref, held_ref, hidden_ref, total_ref, sems = refs[9:]
    width = out_ref.shape[1]
    block = width // SIDE // SIDE

    @pl.when(state_ref[0] == 0)
    def _():
        out_ref[...] = jnp.zeros_like(out_ref)

    @pl.when(state_ref[0] == 1)
    def _():
        ups = [
            pltpu.make_async_copy(up_refs[i], near_ref.at[i], sems.at[SIDE + i])
            for i in range(3)
        ]
        ups += [
            pltpu.make_async_copy(up_refs[3 + i], far_ref.at[i], sems.at[SIDE + 3 + i])
            for i in range(2)
        ]
        for copy in ups:
            copy.start()
        copies = [
            pltpu.make_async_copy(down_refs[i], held_ref.at[i], sems.at[i])
            for i in range(SIDE)
        ]
        for copy in copies:
            copy.start()
        rows = pair_ref[0].astype(jnp.float32) + pair_ref[1].astype(jnp.float32)
        scale = lax.rsqrt(jnp.mean(rows * rows, axis=1, keepdims=True) + 1e-06)
        normed = (rows * scale).astype(jnp.bfloat16)
        y, x = state_ref[2], state_ref[3]
        for index, offset in enumerate(OFFSETS[:3]):
            ups[index].wait()
            part = product(normed, near_ref[index])
            hidden_ref[lax.rem(y + offset, SIDE)] = jax.nn.gelu(part)
        far = lax.rem(y + 2, SIDE)
        ups[3].wait()
        hidden_ref[far, :, :block] = jax.nn.gelu(product(normed, far_ref[0]))
        ups[4].wait()
        hidden_ref[far, :, block:] = jax.nn.gelu(product(normed, far_ref[1]))
        hidden = jnp.concatenate([hidden_ref[i] for i in range(SIDE)], axis=1)
        hidden = hidden.astype(jnp.bfloat16)

        mate = x + 1 - 2 * lax.rem(x, 2)
        for index, at in enumerate((x, mate, SIDE - 1 - x, SIDE - 1 - mate)):
            copies[index].wait()
            total_ref[at] = product(hidden, held_ref[index])
        base = jnp.where(state_ref[1] == 1, rows, 0.0)
        pieces = []
        for i in range(SIDE):
            for j in range(SIDE):
                pieces.append(total_ref[j][:, i * block : (i + 1) * block])
        total = jnp.concatenate(pieces, axis=1)
        out_ref[...] = (base + total).astype(jnp.bfloat16)


def apply_quarter(state, pair, up, down):
    _, row_count, width = pair.shape
    units = down[0].shape[1]
    resident = pl.BlockSpec(memory_space=pltpu.VMEM)
    anywhere = pl.BlockSpec(memory_space=pl.ANY)
    up = [pltpu.with_memory_space_constraint(piece, pltpu.HBM) for piece in up]
    down = [pltpu.with_memory_space_constraint(piece, pltpu.HBM) for piece in down]
    return pl.pallas_call(
        quarter_layer,
        out_shape=jax.ShapeDtypeStruct((row_count, width), jnp.bfloat16),
        in_specs=[pl.BlockSpec(memory_space=pltpu.SMEM)]
        + [resident]
        + [anywhere] * 9,
        out_specs=resident,
        scratch_shapes=[
            pltpu.VMEM((3,) + up[0].shape, jnp.bfloat16),
            pltpu.VMEM((2,) + up[3].shape, jnp.bfloat16),
            pltpu.VMEM((SIDE,) + down[0].shape, jnp.bfloat16),
            pltpu.VMEM((SIDE, row_count, units // SIDE), jnp.float32),
            pltpu.VMEM((SIDE, row_count, width // SIDE), jnp.float32),
            pltpu.SemaphoreType.DMA((SIDE + 5,)),
        ],
        compiler_params=pltpu.CompilerParams(vmem_limit_bytes=32 * 2**20),
        cost_estimate=pl.CostEstimate(
            flops=4 * row_count * width * units,
            bytes_accessed=2 * width * units,
            transcendentals=row_count * units,
        ),
        name="quarter_layer",
    )(state, pair, *up, *down)


def by_halves(low, block, other):
    first = jnp.where(low == 1, block, other)
    second = jnp.where(low == 1, other, block)
    return jnp.concatenate([first, second], axis=0)


def next_plane(layer):
    route = []
    for x, across in INTER:
        for core in range(2):
            to_chip = (x if x < 2 else across) if core == 0 else (x if x >= 2 else across)
            to_core = 0 if x < 2 else 1
            source = (layer * 2 + core) * SIDE + x
            route.append((source, ((layer + 1) * 2 + to_core) * SIDE + to_chip))
    return route


def on_device(layers, patches, w_in, w_out, w_proj):
    plane, core = lax.axis_index("z"), lax.axis_index("c")
    y, x = lax.axis_index("y"), lax.axis_index("x")
    tp = ("y", "x")
    own, wide = w_out.shape[1], w_out.shape[2]
    low = (x < 2).astype(jnp.int32)

    mate = lax.ppermute(w_in[0], "x", INTRA)
    near = by_halves((lax.rem(x, 2) == 0).astype(jnp.int32), w_in[0], mate)

    columns = w_out[0].reshape(own, SIDE, 2, wide // SIDE // 2)
    left = columns[:, :, 0].reshape(own, wide // 2)
    right = columns[:, :, 1].reshape(own, wide // 2)
    both = jnp.stack(
        [jnp.where(low == 1, left, right), jnp.where(low == 1, right, left)]
    )
    below, above, head, tail = ring(both, "y", lambda t: (t[0], t[1]))
    mine = in_order((both[0], below[0], above[0], head), y)
    other = in_order((both[1], below[1], above[1], tail), y)

    flat = patches.reshape(-1, patches.shape[2])
    rows = lax.all_to_all(flat, tp, split_axis=0, concat_axis=1, tiled=True)
    rows = by_halves(low, rows, lax.ppermute(rows, "x", INTER))
    other, rows = lax.optimization_barrier((other, rows))

    across = lax.ppermute(other, "x", INTER)
    beside = lax.ppermute(mine, "x", INTRA)
    corner = lax.ppermute(across, "x", INTRA)
    down = [mine, beside, across, corner]
    near, tail = lax.optimization_barrier((near, tail))
    half = near.shape[0] // 2
    up = [near, *ring(near, "y", lambda t: (t[:half], t[half:]))]
    projection = lax.all_gather(w_proj, tp, axis=0, tiled=True)

    adds = jnp.logical_and(core == 0, low == 1)
    pair = jnp.stack([rows, jnp.zeros_like(rows)])
    for layer in range(layers):
        state = jnp.stack([plane == layer, adds, y, x]).astype(jnp.int32)
        part = apply_quarter(state, pair, up, down)
        cores = lax.all_gather(part, "c", axis=0, tiled=False)
        part = cores[0].astype(jnp.float32) + cores[1].astype(jnp.float32)
        part = part.astype(jnp.bfloat16)
        if layer < layers - 1:
            part = lax.ppermute(part, ("z", "c", "x"), next_plane(layer))
            pair = lax.all_gather(part, "c", axis=0, tiled=False)

    count = part.shape[0] // 2
    kept = jnp.where(low == 1, part[:count], part[count:])
    sent = jnp.where(low == 1, part[count:], part[:count])
    got = lax.ppermute(sent, "x", INTER)
    total = kept.astype(jnp.float32) + got.astype(jnp.float32)
    rows = jnp.where(plane == layers - 1, total, 0.0).astype(jnp.bfloat16)
    holders = [layers - 1]
    step = layers // 2
    while step:
        route = [(held, (held + step) % layers) for held in holders]
        rows = rows + lax.ppermute(rows, "z", route)
        holders += [target for _, target in route]
        step //= 2
    return jnp.dot(rows, projection, preferred_element_type=jnp.float32).astype(
        jnp.bfloat16
    )


def solution(mesh):
    sections = mesh.shape["section"]
    grid = Mesh(
        mesh.devices.reshape(sections // 2, 2, SIDE, SIDE), ("z", "c", "y", "x")
    )
    section, tp = ("z", "c"), ("y", "x")
    return jax.shard_map(
        functools.partial(on_device, sections // 2),
        mesh=grid,
        in_specs=(
            P(None, None, tp),
            P(section, tp, None),
            P(section, tp, None),
            P(tp, section),
        ),
        out_specs=P(tp, section),
        check_vma=False,
    )
```

```python
import functools

import jax
import jax.numpy as jnp
from jax import lax
from jax.experimental import pallas as pl
from jax.experimental.pallas import tpu as pltpu
from jax.sharding import Mesh, PartitionSpec as P

SIDE = 4
OFFSETS = (0, 3, 1, 2)
INTRA = [(0, 1), (1, 0), (2, 3), (3, 2)]
INTER = [(0, 3), (3, 0), (1, 2), (2, 1)]


def moved(block, axis, by):
    route = [(i, (i + by) % SIDE) for i in range(SIDE)]
    return lax.ppermute(block, axis, route)


def ring(block, axis, halves):
    below = moved(block, axis, 1)
    above = moved(block, axis, -1)
    head = moved(halves(below)[0], axis, 1)
    tail = moved(halves(above)[1], axis, -1)
    return below, above, head, tail


def in_order(parts, place):
    whole = jnp.zeros((SIDE,) + parts[0].shape, parts[0].dtype)
    for part, offset in zip(parts, OFFSETS):
        at = lax.rem(place + offset, SIDE)
        whole = lax.dynamic_update_slice(whole, part[None], (at, 0, 0))
    return whole


def run_all(copies):
    for copy in copies:
        copy.start()
    for copy in copies:
        copy.wait()


def early(spots_ref, *refs):
    sources, (up_ref, down_ref, sems) = refs[:6], refs[6:]
    copies = []
    for i in range(3):
        to_up, to_down = up_ref.at[spots_ref[i]], down_ref.at[spots_ref[SIDE + i]]
        copies.append(pltpu.make_async_copy(sources[i], to_up, sems.at[i]))
        copies.append(pltpu.make_async_copy(sources[3 + i], to_down, sems.at[3 + i]))
    run_all(copies)


def late(spots_ref, head_ref, tail_ref, corner_ref, *refs):
    up_ref, down_ref, sems = refs[2:]
    cut, whole = head_ref.shape[1], up_ref.shape[2]
    far = up_ref.at[spots_ref[SIDE - 1]]
    corner = down_ref.at[spots_ref[2 * SIDE - 1]]
    copies = [
        pltpu.make_async_copy(head_ref, far.at[:, :cut], sems.at[0]),
        pltpu.make_async_copy(tail_ref, far.at[:, cut:whole], sems.at[1]),
        pltpu.make_async_copy(corner_ref, corner, sems.at[2]),
    ]
    run_all(copies)


def put_early(spots, *pieces):
    kind = pieces[0].dtype
    anywhere = pl.BlockSpec(memory_space=pl.ANY)
    return pl.pallas_call(
        early,
        out_shape=(
            jax.ShapeDtypeStruct((SIDE,) + pieces[0].shape, kind),
            jax.ShapeDtypeStruct((SIDE,) + pieces[3].shape, kind),
        ),
        in_specs=[pl.BlockSpec(memory_space=pltpu.SMEM)] + [anywhere] * 6,
        out_specs=(anywhere, anywhere),
        scratch_shapes=[pltpu.SemaphoreType.DMA((6,))],
        compiler_params=pltpu.CompilerParams(vmem_limit_bytes=2**20),
        name="put_early",
    )(spots, *pieces)


def put_late(spots, head, tail, corner, up, down):
    anywhere = pl.BlockSpec(memory_space=pl.ANY)
    return pl.pallas_call(
        late,
        out_shape=(
            jax.ShapeDtypeStruct(up.shape, up.dtype),
            jax.ShapeDtypeStruct(down.shape, down.dtype),
        ),
        in_specs=[pl.BlockSpec(memory_space=pltpu.SMEM)] + [anywhere] * 5,
        out_specs=(anywhere, anywhere),
        scratch_shapes=[pltpu.SemaphoreType.DMA((3,))],
        input_output_aliases={4: 0, 5: 1},
        compiler_params=pltpu.CompilerParams(vmem_limit_bytes=2**20),
        name="put_late",
    )(spots, head, tail, corner, up, down)


def product(left, right):
    return lax.dot_general(
        left, right, (((1,), (1,)), ((), ())), preferred_element_type=jnp.float32
    )


def quarter_layer(tick_ref, state_ref, pair_ref, up_ref, down_ref, out_ref, *scratch):
    hidden_ref, total_ref = scratch
    width = out_ref.shape[1]
    step = up_ref.shape[1]
    block = width // SIDE // SIDE
    active = tick_ref[0] == state_ref[0]

    @pl.when(jnp.logical_not(active))
    def _():
        out_ref[...] = jnp.zeros_like(out_ref)

    @pl.when(active)
    def _():
        rows = pair_ref[0].astype(jnp.float32) + pair_ref[1].astype(jnp.float32)
        scale = lax.rsqrt(jnp.mean(rows * rows, axis=1, keepdims=True) + 1e-06)
        normed = (rows * scale).astype(jnp.bfloat16)
        for i in range(SIDE):
            part = jax.nn.gelu(product(normed, up_ref[i])).astype(jnp.bfloat16)
            hidden_ref[:, i * step : (i + 1) * step] = part
        hidden = hidden_ref[...]
        for i in range(SIDE):
            total_ref[i] = product(hidden, down_ref[i])
        base = jnp.where(state_ref[1] == 1, rows, 0.0)
        pieces = []
        for i in range(SIDE):
            for j in range(SIDE):
                pieces.append(total_ref[j][:, i * block : (i + 1) * block])
        total = jnp.concatenate(pieces, axis=1)
        out_ref[...] = (base + total).astype(jnp.bfloat16)


def apply_quarter(tick, state, pair, up, down):
    _, row_count, width = pair.shape
    units = down.shape[2]
    resident = pl.BlockSpec(memory_space=pltpu.VMEM)
    scalar = pl.BlockSpec(memory_space=pltpu.SMEM)
    return pl.pallas_call(
        quarter_layer,
        out_shape=jax.ShapeDtypeStruct((row_count, width), jnp.bfloat16),
        in_specs=[scalar] * 2 + [resident] * 3,
        out_specs=resident,
        scratch_shapes=[
            pltpu.VMEM((row_count, units), jnp.bfloat16),
            pltpu.VMEM((SIDE, row_count, width // SIDE), jnp.float32),
        ],
        compiler_params=pltpu.CompilerParams(vmem_limit_bytes=10 * 2**20),
        cost_estimate=pl.CostEstimate(
            flops=4 * row_count * width * units,
            bytes_accessed=4 * row_count * width,
            transcendentals=row_count * units,
        ),
        name="quarter_layer",
    )(tick, state, pair, up, down)


def add_pair(pair_ref, out_ref):
    total = pair_ref[0].astype(jnp.float32) + pair_ref[1].astype(jnp.float32)
    out_ref[...] = total.astype(out_ref.dtype)


def added(pair):
    resident = pl.BlockSpec(memory_space=pltpu.VMEM)
    return pl.pallas_call(
        add_pair,
        out_shape=jax.ShapeDtypeStruct(pair.shape[1:], pair.dtype),
        in_specs=[resident],
        out_specs=resident,
        compiler_params=pltpu.CompilerParams(vmem_limit_bytes=2 * 2**20),
        cost_estimate=pl.CostEstimate(
            flops=pair.size, bytes_accessed=pair.size, transcendentals=0
        ),
        name="add_pair",
    )(pair)


def split_columns(low_ref, block_ref, out_ref):
    width = block_ref.shape[1] // SIDE // 2
    low = low_ref[0] == 1
    for i in range(SIDE):
        left = block_ref[:, 2 * i * width : (2 * i + 1) * width]
        right = block_ref[:, (2 * i + 1) * width : (2 * i + 2) * width]
        out_ref[0, :, i * width : (i + 1) * width] = jnp.where(low, left, right)
        out_ref[1, :, i * width : (i + 1) * width] = jnp.where(low, right, left)


def own_and_other(low, block):
    rows, width = block.shape
    resident = pl.BlockSpec(memory_space=pltpu.VMEM)
    return pl.pallas_call(
        split_columns,
        out_shape=jax.ShapeDtypeStruct((2, rows, width // 2), block.dtype),
        in_specs=[pl.BlockSpec(memory_space=pltpu.SMEM), resident],
        out_specs=resident,
        compiler_params=pltpu.CompilerParams(vmem_limit_bytes=10 * 2**20),
        name="split_columns",
    )(low.reshape(1), block)


def by_halves(low, block, other):
    first = jnp.where(low == 1, block, other)
    second = jnp.where(low == 1, other, block)
    return jnp.concatenate([first, second], axis=0)


def next_plane(layer):
    route = []
    for x, across in INTER:
        for core in range(2):
            to_chip = (x if x < 2 else across) if core == 0 else (x if x >= 2 else across)
            to_core = 0 if x < 2 else 1
            source = (layer * 2 + core) * SIDE + x
            route.append((source, ((layer + 1) * 2 + to_core) * SIDE + to_chip))
    return route


def on_device(layers, patches, w_in, w_out, w_proj):
    plane, core = lax.axis_index("z"), lax.axis_index("c")
    y, x = lax.axis_index("y"), lax.axis_index("x")
    tp = ("y", "x")
    low = (x < 2).astype(jnp.int32)

    mate = lax.ppermute(w_in[0], "x", INTRA)
    near = by_halves((lax.rem(x, 2) == 0).astype(jnp.int32), w_in[0], mate)

    both = own_and_other(low, w_out[0])
    below, above, head, tail = ring(both, "y", lambda t: (t[0], t[1]))
    mine = in_order((both[0], below[0], above[0], head), y)
    other = in_order((both[1], below[1], above[1], tail), y)

    flat = patches.reshape(-1, patches.shape[2])
    rows = lax.all_to_all(flat, tp, split_axis=0, concat_axis=1, tiled=True)
    rows = by_halves(low, rows, lax.ppermute(rows, "x", INTER))
    other, rows = lax.optimization_barrier((other, rows))

    mine = mine.reshape(-1, mine.shape[2])
    other = other.reshape(mine.shape)
    across = lax.ppermute(other, "x", INTER)
    beside = lax.ppermute(mine, "x", INTRA)
    corner = lax.ppermute(across, "x", INTRA)
    mate_x = x + 1 - 2 * lax.rem(x, 2)
    near, head, tail = lax.optimization_barrier((near, head, tail))
    cut = near.shape[1] // 256 * 128
    below, above, head, tail = ring(near, "y", lambda t: (t[:, :cut], t[:, cut:]))
    spots = [y, lax.rem(y + 3, SIDE), lax.rem(y + 1, SIDE), lax.rem(y + 2, SIDE)]
    spots += [x, mate_x, SIDE - 1 - x, SIDE - 1 - mate_x]
    spots = jnp.stack(spots).astype(jnp.int32)
    up, down = put_early(spots, near, below, above, mine, beside, across)
    up, down = put_late(spots, head, tail, corner, up, down)
    up = pltpu.with_memory_space_constraint(up, pltpu.VMEM)
    down = pltpu.with_memory_space_constraint(down, pltpu.VMEM)
    projection = lax.all_gather(w_proj, tp, axis=0, tiled=True)

    adds = jnp.logical_and(core == 0, low == 1)
    state = jnp.stack([plane, adds]).astype(jnp.int32)
    pair = jnp.stack([rows, jnp.zeros_like(rows)])
    pair, state, projection = lax.optimization_barrier((pair, state, projection))
    for layer in range(layers):
        tick = jnp.full((1,), layer, jnp.int32)
        part = apply_quarter(tick, state, pair, up, down)
        part = added(lax.all_gather(part, "c", axis=0, tiled=False))
        if layer < layers - 1:
            part = lax.ppermute(part, ("z", "c", "x"), next_plane(layer))
            pair = lax.all_gather(part, "c", axis=0, tiled=False)

    count = part.shape[0] // 2
    kept = jnp.where(low == 1, part[:count], part[count:])
    sent = jnp.where(low == 1, part[count:], part[:count])
    got = lax.ppermute(sent, "x", INTER)
    total = kept.astype(jnp.float32) + got.astype(jnp.float32)
    rows = jnp.where(plane == layers - 1, total, 0.0).astype(jnp.bfloat16)
    holders = [layers - 1]
    step = layers // 2
    while step:
        route = [(held, (held + step) % layers) for held in holders]
        rows = rows + lax.ppermute(rows, "z", route)
        holders += [target for _, target in route]
        step //= 2
    return jnp.dot(rows, projection, preferred_element_type=jnp.float32).astype(
        jnp.bfloat16
    )


def solution(mesh):
    sections = mesh.shape["section"]
    grid = Mesh(
        mesh.devices.reshape(sections // 2, 2, SIDE, SIDE), ("z", "c", "y", "x")
    )
    section, tp = ("z", "c"), ("y", "x")
    return jax.shard_map(
        functools.partial(on_device, sections // 2),
        mesh=grid,
        in_specs=(
            P(None, None, tp),
            P(section, tp, None),
            P(section, tp, None),
            P(tp, section),
        ),
        out_specs=P(tp, section),
        check_vma=False,
    )
```

```python
import functools

import jax
import jax.numpy as jnp
from jax import lax
from jax.experimental import pallas as pl
from jax.experimental.pallas import tpu as pltpu
from jax.sharding import Mesh, PartitionSpec as P

SIDE = 4
OFFSETS = (0, 3, 1, 2)
INTRA = [(0, 1), (1, 0), (2, 3), (3, 2)]
INTER = [(0, 3), (3, 0), (1, 2), (2, 1)]


def moved(block, axis, by):
    route = [(i, (i + by) % SIDE) for i in range(SIDE)]
    return lax.ppermute(block, axis, route)


def ring(first, second, axis):
    first_below = moved(first, axis, 1)
    second_above = moved(second, axis, -1)
    second_below = moved(second, axis, 1)
    first_above = moved(first, axis, -1)
    first_far = moved(first_below, axis, 1)
    second_far = moved(second_above, axis, -1)
    return (first_below, first_above, first_far), (second_below, second_above, second_far)


def run_all(copies):
    for copy in copies:
        copy.start()
    for copy in copies:
        copy.wait()


def put(plan, spots_ref, *refs):
    sources, targets, sems = refs[: len(plan)], refs[-5:-1], refs[-1]
    run_all(
        [
            pltpu.make_async_copy(source, targets[to].at[spots_ref[spot]], sems.at[i])
            for i, (source, (to, spot)) in enumerate(zip(sources, plan))
        ]
    )


def put_pieces(spots, plan, pieces, targets, shapes):
    anywhere = pl.BlockSpec(memory_space=pl.ANY)
    count = len(pieces)
    return pl.pallas_call(
        functools.partial(put, plan),
        out_shape=tuple(jax.ShapeDtypeStruct(s, pieces[0].dtype) for s in shapes),
        in_specs=[pl.BlockSpec(memory_space=pltpu.SMEM)]
        + [anywhere] * (count + len(targets)),
        out_specs=(anywhere,) * 4,
        scratch_shapes=[pltpu.SemaphoreType.DMA((count,))],
        input_output_aliases={1 + count + i: i for i in range(len(targets))},
        compiler_params=pltpu.CompilerParams(vmem_limit_bytes=2**20),
        name="put_pieces",
    )(spots, *pieces, *targets)


def product(left, right):
    return lax.dot_general(
        left, right, (((1,), (1,)), ((), ())), preferred_element_type=jnp.float32
    )


def quarter_layer(tick_ref, state_ref, pair_ref, *refs):
    left_ref, right_ref, own_ref, rest_ref, out_ref, hidden_ref, total_ref = refs
    step, cut = left_ref.shape[1:]
    block = own_ref.shape[1]
    active = tick_ref[0] == state_ref[0]

    @pl.when(jnp.logical_not(active))
    def _():
        out_ref[...] = jnp.zeros_like(out_ref)

    @pl.when(active)
    def _():
        rows = pair_ref[0].astype(jnp.float32) + pair_ref[1].astype(jnp.float32)
        scale = lax.rsqrt(jnp.mean(rows * rows, axis=1, keepdims=True) + 1e-06)
        normed = (rows * scale).astype(jnp.bfloat16)
        for i in range(SIDE):
            part = product(normed[:, :cut], left_ref[i])
            part = part + product(normed[:, cut:], right_ref[i])
            part = jax.nn.gelu(part).astype(jnp.bfloat16)
            hidden_ref[:, i * step : (i + 1) * step] = part
        hidden = hidden_ref[...]
        places = [lax.rem(state_ref[2] + offset, SIDE) for offset in OFFSETS]
        for i in range(SIDE):
            total_ref[i, places[0]] = product(hidden, own_ref[i])
            part = product(hidden, rest_ref[i])
            for j in range(SIDE - 1):
                total_ref[i, places[1 + j]] = part[:, j * block : (j + 1) * block]
        pieces = [total_ref[j, i] for i in range(SIDE) for j in range(SIDE)]
        total = jnp.concatenate(pieces, axis=1)
        base = jnp.where(state_ref[1] == 1, rows, 0.0)
        out_ref[...] = (base + total).astype(jnp.bfloat16)


def apply_quarter(tick, state, pair, weights):
    _, row_count, width = pair.shape
    units, block = weights[2].shape[2], weights[2].shape[1]
    resident = pl.BlockSpec(memory_space=pltpu.VMEM)
    scalar = pl.BlockSpec(memory_space=pltpu.SMEM)
    return pl.pallas_call(
        quarter_layer,
        out_shape=jax.ShapeDtypeStruct((row_count, width), jnp.bfloat16),
        in_specs=[scalar] * 2 + [resident] * 5,
        out_specs=resident,
        scratch_shapes=[
            pltpu.VMEM((row_count, units), jnp.bfloat16),
            pltpu.VMEM((SIDE, SIDE, row_count, block), jnp.float32),
        ],
        compiler_params=pltpu.CompilerParams(vmem_limit_bytes=10 * 2**20),
        cost_estimate=pl.CostEstimate(
            flops=4 * row_count * width * units,
            bytes_accessed=4 * row_count * width,
            transcendentals=row_count * units,
        ),
        name="quarter_layer",
    )(tick, state, pair, *weights)


def add_pair(pair_ref, out_ref):
    total = pair_ref[0].astype(jnp.float32) + pair_ref[1].astype(jnp.float32)
    out_ref[...] = total.astype(out_ref.dtype)


def added(pair):
    resident = pl.BlockSpec(memory_space=pltpu.VMEM)
    return pl.pallas_call(
        add_pair,
        out_shape=jax.ShapeDtypeStruct(pair.shape[1:], pair.dtype),
        in_specs=[resident],
        out_specs=resident,
        compiler_params=pltpu.CompilerParams(vmem_limit_bytes=2 * 2**20),
        cost_estimate=pl.CostEstimate(
            flops=pair.size, bytes_accessed=pair.size, transcendentals=0
        ),
        name="add_pair",
    )(pair)


def split_columns(low_ref, block_ref, own_ref, other_ref):
    width = block_ref.shape[1] // SIDE // 2
    low = low_ref[0] == 1
    for i in range(SIDE):
        left = block_ref[:, 2 * i * width : (2 * i + 1) * width]
        right = block_ref[:, (2 * i + 1) * width : (2 * i + 2) * width]
        own_ref[:, i * width : (i + 1) * width] = jnp.where(low, left, right)
        other_ref[:, i * width : (i + 1) * width] = jnp.where(low, right, left)


def own_and_other(low, block):
    rows, width = block.shape
    resident = pl.BlockSpec(memory_space=pltpu.VMEM)
    half = jax.ShapeDtypeStruct((rows, width // 2), block.dtype)
    return pl.pallas_call(
        split_columns,
        out_shape=(half, half),
        in_specs=[pl.BlockSpec(memory_space=pltpu.SMEM), resident],
        out_specs=(resident, resident),
        compiler_params=pltpu.CompilerParams(vmem_limit_bytes=10 * 2**20),
        name="split_columns",
    )(low.reshape(1), block)


def by_halves(low, block, other):
    first = jnp.where(low == 1, block, other)
    second = jnp.where(low == 1, other, block)
    return jnp.concatenate([first, second], axis=0)


def next_plane(layer):
    route = []
    for x, across in INTER:
        for core in range(2):
            to_chip = (x if x < 2 else across) if core == 0 else (x if x >= 2 else across)
            to_core = 0 if x < 2 else 1
            source = (layer * 2 + core) * SIDE + x
            route.append((source, ((layer + 1) * 2 + to_core) * SIDE + to_chip))
    return route


def on_device(layers, patches, w_in, w_out, w_proj):
    plane, core = lax.axis_index("z"), lax.axis_index("c")
    y, x = lax.axis_index("y"), lax.axis_index("x")
    tp = ("y", "x")
    low = (x < 2).astype(jnp.int32)

    own, other = own_and_other(low, w_out[0])
    mate = lax.ppermute(w_in[0], "x", INTRA)
    own_ring, other_ring = ring(own, other, "y")
    beside = lax.ppermute(own, "x", INTRA)
    across = lax.ppermute(other, "x", INTER)
    corner = lax.ppermute(across, "x", INTRA)
    held = (own_ring, other_ring, beside, across, corner)
    own_ring, other_ring, beside, across, corner = lax.optimization_barrier(held)
    own_rest = jnp.concatenate(own_ring, axis=0)
    other_rest = jnp.concatenate(other_ring, axis=0)

    even = (lax.rem(x, 2) == 0).astype(jnp.int32)
    cut = w_in.shape[2] // 256 * 128
    left = by_halves(even, w_in[0, :, :cut], mate[:, :cut])
    right = by_halves(even, w_in[0, :, cut:], mate[:, cut:])
    held = (left, right, own_rest, other_rest)
    left, right, own_rest, other_rest = lax.optimization_barrier(held)
    beside_rest = lax.ppermute(own_rest, "x", INTRA)
    across_rest = lax.ppermute(other_rest, "x", INTER)
    left_ring, right_ring = ring(left, right, "y")
    across_rest, patches = lax.optimization_barrier((across_rest, patches))
    corner_rest = lax.ppermute(across_rest, "x", INTRA)

    flat = patches.reshape(-1, patches.shape[2])
    rows = lax.all_to_all(flat, tp, split_axis=0, concat_axis=1, tiled=True)
    rows = by_halves(low, rows, lax.ppermute(rows, "x", INTER))

    mate_x = x + 1 - 2 * lax.rem(x, 2)
    spots = [lax.rem(y + offset, SIDE) for offset in OFFSETS]
    spots += [x, mate_x, SIDE - 1 - x, SIDE - 1 - mate_x]
    spots = jnp.stack(spots).astype(jnp.int32)
    projection = lax.all_gather(w_proj, tp, axis=0, tiled=True)
    adds = jnp.logical_and(core == 0, low == 1)
    state = jnp.stack([plane, adds, y]).astype(jnp.int32)
    pair = jnp.stack([rows, jnp.zeros_like(rows)])
    held = (spots, pair, state, projection)
    spots, pair, state, projection = lax.optimization_barrier(held)
    early = [(left, 0, 0), (left_ring[0], 0, 1), (left_ring[1], 0, 2)]
    early += [(right, 1, 0), (right_ring[0], 1, 1), (right_ring[1], 1, 2)]
    early += [(own, 2, 4), (beside, 2, 5), (across, 2, 6), (corner, 2, 7)]
    early += [(own_rest, 3, 4), (beside_rest, 3, 5), (across_rest, 3, 6)]
    late = [(left_ring[2], 0, 3), (right_ring[2], 1, 3), (corner_rest, 3, 7)]
    shapes = [(SIDE,) + piece.shape for piece in (left, right, own, own_rest)]
    weights = ()
    for group in (early, late):
        plan = tuple((to, spot) for _, to, spot in group)
        pieces = [piece for piece, _, _ in group]
        weights = put_pieces(spots, plan, pieces, weights, shapes)
    weights = [pltpu.with_memory_space_constraint(w, pltpu.VMEM) for w in weights]
    for layer in range(layers):
        tick = jnp.full((1,), layer, jnp.int32)
        part = apply_quarter(tick, state, pair, weights)
        part = added(lax.all_gather(part, "c", axis=0, tiled=False))
        if layer < layers - 1:
            part = lax.ppermute(part, ("z", "c", "x"), next_plane(layer))
            pair = lax.all_gather(part, "c", axis=0, tiled=False)

    count = part.shape[0] // 2
    kept = jnp.where(low == 1, part[:count], part[count:])
    sent = jnp.where(low == 1, part[count:], part[:count])
    last = (layers - 1) * SIDE
    route = [(last + here, last + there) for here, there in INTER]
    got = lax.ppermute(sent, ("z", "x"), route)
    total = kept.astype(jnp.float32) + got.astype(jnp.float32)
    rows = jnp.where(plane == layers - 1, total, 0.0).astype(jnp.bfloat16)
    holders = [layers - 1]
    step = layers // 2
    while step:
        route = [(held, (held + step) % layers) for held in holders]
        rows = rows + lax.ppermute(rows, "z", route)
        holders += [target for _, target in route]
        step //= 2
    return jnp.dot(rows, projection, preferred_element_type=jnp.float32).astype(
        jnp.bfloat16
    )


def solution(mesh):
    sections = mesh.shape["section"]
    grid = Mesh(
        mesh.devices.reshape(sections // 2, 2, SIDE, SIDE), ("z", "c", "y", "x")
    )
    section, tp = ("z", "c"), ("y", "x")
    return jax.shard_map(
        functools.partial(on_device, sections // 2),
        mesh=grid,
        in_specs=(
            P(None, None, tp),
            P(section, tp, None),
            P(section, tp, None),
            P(tp, section),
        ),
        out_specs=P(tp, section),
        check_vma=False,
    )
```

```python
import functools

import jax
import jax.numpy as jnp
from jax import lax
from jax.experimental import pallas as pl
from jax.experimental.pallas import tpu as pltpu
from jax.sharding import Mesh, PartitionSpec as P

SIDE = 4
OFFSETS = (0, 3, 1, 2)
INTRA = [(0, 1), (1, 0), (2, 3), (3, 2)]
INTER = [(0, 3), (3, 0), (1, 2), (2, 1)]


def moved(block, axis, by):
    route = [(i, (i + by) % SIDE) for i in range(SIDE)]
    return lax.ppermute(block, axis, route)


def ring(first, second, axis):
    first_below = moved(first, axis, 1)
    second_above = moved(second, axis, -1)
    second_below = moved(second, axis, 1)
    first_above = moved(first, axis, -1)
    first_far = moved(first_below, axis, 1)
    second_far = moved(second_above, axis, -1)
    return (first_below, first_above, first_far), (second_below, second_above, second_far)


def run_all(copies):
    for copy in copies:
        copy.start()
    for copy in copies:
        copy.wait()


def put(plan, spots_ref, *refs):
    count = len(plan)
    sources, targets, sems = refs[:count], refs[-4:-1], refs[-1]
    copies = []
    for i, (to, spot, start) in enumerate(plan):
        place = targets[to].at[spots_ref[spot]]
        width = sources[i].shape[1]
        if width != targets[to].shape[2]:
            place = place.at[:, start : start + width]
        copies.append(pltpu.make_async_copy(sources[i], place, sems.at[i]))
    run_all(copies)


def put_pieces(spots, plan, pieces, targets, shapes):
    anywhere = pl.BlockSpec(memory_space=pl.ANY)
    count = len(pieces)
    return pl.pallas_call(
        functools.partial(put, plan),
        out_shape=tuple(jax.ShapeDtypeStruct(s, pieces[0].dtype) for s in shapes),
        in_specs=[pl.BlockSpec(memory_space=pltpu.SMEM)]
        + [anywhere] * (count + len(targets)),
        out_specs=(anywhere,) * 3,
        scratch_shapes=[pltpu.SemaphoreType.DMA((count,))],
        input_output_aliases={1 + count + i: i for i in range(len(targets))},
        compiler_params=pltpu.CompilerParams(vmem_limit_bytes=2**20),
        name="put_pieces",
    )(spots, *pieces, *targets)


def product(left, right):
    return lax.dot_general(
        left, right, (((1,), (1,)), ((), ())), preferred_element_type=jnp.float32
    )


def quarter_layer(tick_ref, state_ref, pair_ref, *refs):
    up_ref, own_ref, rest_ref, out_ref, hidden_ref, total_ref = refs
    step = up_ref.shape[1]
    block = own_ref.shape[1]
    active = tick_ref[0] == state_ref[0]

    @pl.when(jnp.logical_not(active))
    def _():
        out_ref[...] = jnp.zeros_like(out_ref)

    @pl.when(active)
    def _():
        rows = pair_ref[0].astype(jnp.float32) + pair_ref[1].astype(jnp.float32)
        scale = lax.rsqrt(jnp.mean(rows * rows, axis=1, keepdims=True) + 1e-06)
        normed = (rows * scale).astype(jnp.bfloat16)
        for i in range(SIDE):
            part = jax.nn.gelu(product(normed, up_ref[i])).astype(jnp.bfloat16)
            hidden_ref[:, i * step : (i + 1) * step] = part
        hidden = hidden_ref[...]
        places = [lax.rem(state_ref[2] + offset, SIDE) for offset in OFFSETS]
        for i in range(SIDE):
            total_ref[i, places[0]] = product(hidden, own_ref[i])
            part = product(hidden, rest_ref[i])
            for j in range(SIDE - 1):
                total_ref[i, places[1 + j]] = part[:, j * block : (j + 1) * block]
        pieces = [total_ref[j, i] for i in range(SIDE) for j in range(SIDE)]
        total = jnp.concatenate(pieces, axis=1)
        base = jnp.where(state_ref[1] == 1, rows, 0.0)
        out_ref[...] = (base + total).astype(jnp.bfloat16)


def apply_quarter(tick, state, pair, weights):
    _, row_count, width = pair.shape
    units, block = weights[1].shape[2], weights[1].shape[1]
    resident = pl.BlockSpec(memory_space=pltpu.VMEM)
    scalar = pl.BlockSpec(memory_space=pltpu.SMEM)
    return pl.pallas_call(
        quarter_layer,
        out_shape=jax.ShapeDtypeStruct((row_count, width), jnp.bfloat16),
        in_specs=[scalar] * 2 + [resident] * 4,
        out_specs=resident,
        scratch_shapes=[
            pltpu.VMEM((row_count, units), jnp.bfloat16),
            pltpu.VMEM((SIDE, SIDE, row_count, block), jnp.float32),
        ],
        compiler_params=pltpu.CompilerParams(vmem_limit_bytes=10 * 2**20),
        cost_estimate=pl.CostEstimate(
            flops=4 * row_count * width * units,
            bytes_accessed=4 * row_count * width,
            transcendentals=row_count * units,
        ),
        name="quarter_layer",
    )(tick, state, pair, *weights)


def add_pair(pair_ref, out_ref):
    total = pair_ref[0].astype(jnp.float32) + pair_ref[1].astype(jnp.float32)
    out_ref[...] = total.astype(out_ref.dtype)


def added(pair):
    resident = pl.BlockSpec(memory_space=pltpu.VMEM)
    return pl.pallas_call(
        add_pair,
        out_shape=jax.ShapeDtypeStruct(pair.shape[1:], pair.dtype),
        in_specs=[resident],
        out_specs=resident,
        compiler_params=pltpu.CompilerParams(vmem_limit_bytes=2 * 2**20),
        cost_estimate=pl.CostEstimate(
            flops=pair.size, bytes_accessed=pair.size, transcendentals=0
        ),
        name="add_pair",
    )(pair)


def split_columns(low_ref, block_ref, own_ref, other_ref):
    width = block_ref.shape[1] // SIDE // 2
    low = low_ref[0] == 1
    for i in range(SIDE):
        left = block_ref[:, 2 * i * width : (2 * i + 1) * width]
        right = block_ref[:, (2 * i + 1) * width : (2 * i + 2) * width]
        own_ref[:, i * width : (i + 1) * width] = jnp.where(low, left, right)
        other_ref[:, i * width : (i + 1) * width] = jnp.where(low, right, left)


def own_and_other(low, block):
    rows, width = block.shape
    resident = pl.BlockSpec(memory_space=pltpu.VMEM)
    half = jax.ShapeDtypeStruct((rows, width // 2), block.dtype)
    return pl.pallas_call(
        split_columns,
        out_shape=(half, half),
        in_specs=[pl.BlockSpec(memory_space=pltpu.SMEM), resident],
        out_specs=(resident, resident),
        compiler_params=pltpu.CompilerParams(vmem_limit_bytes=10 * 2**20),
        name="split_columns",
    )(low.reshape(1), block)


def by_halves(low, block, other):
    first = jnp.where(low == 1, block, other)
    second = jnp.where(low == 1, other, block)
    return jnp.concatenate([first, second], axis=0)


def next_plane(layer):
    route = []
    for x, across in INTER:
        for core in range(2):
            to_chip = (x if x < 2 else across) if core == 0 else (x if x >= 2 else across)
            to_core = 0 if x < 2 else 1
            source = (layer * 2 + core) * SIDE + x
            route.append((source, ((layer + 1) * 2 + to_core) * SIDE + to_chip))
    return route


def on_device(layers, patches, w_in, w_out, w_proj):
    plane, core = lax.axis_index("z"), lax.axis_index("c")
    y, x = lax.axis_index("y"), lax.axis_index("x")
    tp = ("y", "x")
    low = (x < 2).astype(jnp.int32)

    own, other = own_and_other(low, w_out[0])
    mate = lax.ppermute(w_in[0], "x", INTRA)
    own_ring, other_ring = ring(own, other, "y")
    beside = lax.ppermute(own, "x", INTRA)
    across = lax.ppermute(other, "x", INTER)
    corner = lax.ppermute(across, "x", INTRA)
    beside, across, patches = lax.optimization_barrier((beside, across, patches))
    flat = patches.reshape(-1, patches.shape[2])
    rows = lax.all_to_all(flat, tp, split_axis=0, concat_axis=1, tiled=True)
    held = (own_ring, other_ring, beside, across, rows)
    own_ring, other_ring, beside, across, rows = lax.optimization_barrier(held)
    own_rest = jnp.concatenate(own_ring, axis=0)
    other_rest = jnp.concatenate(other_ring, axis=0)
    rows = by_halves(low, rows, lax.ppermute(rows, "x", INTER))

    near = by_halves((lax.rem(x, 2) == 0).astype(jnp.int32), w_in[0], mate)
    held = (near, own_rest, other_rest)
    near, own_rest, other_rest = lax.optimization_barrier(held)
    beside_rest = lax.ppermute(own_rest, "x", INTRA)
    across_rest = lax.ppermute(other_rest, "x", INTER)
    corner_rest = lax.ppermute(across_rest, "x", INTRA)
    cut = near.shape[1] // 256 * 128
    below = moved(near, "y", 1)
    above = moved(near, "y", -1)
    head = moved(below[:, :cut], "y", 1)
    tail = moved(above[:, cut:], "y", -1)

    mate_x = x + 1 - 2 * lax.rem(x, 2)
    spots = [lax.rem(y + offset, SIDE) for offset in OFFSETS]
    spots += [x, mate_x, SIDE - 1 - x, SIDE - 1 - mate_x]
    spots = jnp.stack(spots).astype(jnp.int32)
    projection = lax.all_gather(w_proj, tp, axis=0, tiled=True)
    adds = jnp.logical_and(core == 0, low == 1)
    state = jnp.stack([plane, adds, y]).astype(jnp.int32)
    pair = jnp.stack([rows, jnp.zeros_like(rows)])
    held = (spots, pair, state, projection)
    spots, pair, state, projection = lax.optimization_barrier(held)
    early = [(near, 0, 0, 0), (below, 0, 1, 0), (above, 0, 2, 0)]
    early += [(own, 1, 4, 0), (beside, 1, 5, 0), (across, 1, 6, 0), (corner, 1, 7, 0)]
    early += [(own_rest, 2, 4, 0), (beside_rest, 2, 5, 0), (across_rest, 2, 6, 0)]
    late = [(head, 0, 3, 0), (tail, 0, 3, cut), (corner_rest, 2, 7, 0)]
    shapes = [(SIDE,) + piece.shape for piece in (near, own, own_rest)]
    weights = ()
    for group in (early, late):
        plan = tuple(entry[1:] for entry in group)
        pieces = [entry[0] for entry in group]
        weights = put_pieces(spots, plan, pieces, weights, shapes)
    weights = [pltpu.with_memory_space_constraint(w, pltpu.VMEM) for w in weights]
    for layer in range(layers):
        tick = jnp.full((1,), layer, jnp.int32)
        part = apply_quarter(tick, state, pair, weights)
        part = added(lax.all_gather(part, "c", axis=0, tiled=False))
        if layer < layers - 1:
            part = lax.ppermute(part, ("z", "c", "x"), next_plane(layer))
            pair = lax.all_gather(part, "c", axis=0, tiled=False)

    count = part.shape[0] // 2
    kept = jnp.where(low == 1, part[:count], part[count:])
    sent = jnp.where(low == 1, part[count:], part[:count])
    last = (layers - 1) * SIDE
    route = [(last + here, last + there) for here, there in INTER]
    got = lax.ppermute(sent, ("z", "x"), route)
    total = kept.astype(jnp.float32) + got.astype(jnp.float32)
    rows = jnp.where(plane == layers - 1, total, 0.0).astype(jnp.bfloat16)
    holders = [layers - 1]
    step = layers // 2
    while step:
        route = [(held, (held + step) % layers) for held in holders]
        rows = rows + lax.ppermute(rows, "z", route)
        holders += [target for _, target in route]
        step //= 2
    return jnp.dot(rows, projection, preferred_element_type=jnp.float32).astype(
        jnp.bfloat16
    )


def solution(mesh):
    sections = mesh.shape["section"]
    grid = Mesh(
        mesh.devices.reshape(sections // 2, 2, SIDE, SIDE), ("z", "c", "y", "x")
    )
    section, tp = ("z", "c"), ("y", "x")
    return jax.shard_map(
        functools.partial(on_device, sections // 2),
        mesh=grid,
        in_specs=(
            P(None, None, tp),
            P(section, tp, None),
            P(section, tp, None),
            P(tp, section),
        ),
        out_specs=P(tp, section),
        check_vma=False,
    )
```

```python
import functools

import jax
import jax.numpy as jnp
from jax import lax
from jax.experimental import pallas as pl
from jax.experimental.pallas import tpu as pltpu
from jax.sharding import Mesh, PartitionSpec as P

SIDE = 4
OFFSETS = (0, 3, 1, 2)
INTRA = [(0, 1), (1, 0), (2, 3), (3, 2)]
INTER = [(0, 3), (3, 0), (1, 2), (2, 1)]


def moved(block, axis, by):
    route = [(i, (i + by) % SIDE) for i in range(SIDE)]
    return lax.ppermute(block, axis, route)


def ring(first, second, axis):
    first_below = moved(first, axis, 1)
    second_above = moved(second, axis, -1)
    second_below = moved(second, axis, 1)
    first_above = moved(first, axis, -1)
    first_far = moved(first_below, axis, 1)
    second_far = moved(second_above, axis, -1)
    return (first_below, first_above, first_far), (second_below, second_above, second_far)


def run_all(copies):
    for copy in copies:
        copy.start()
    for copy in copies:
        copy.wait()


def put(plan, spots_ref, *refs):
    count = len(plan)
    sources, targets, sems = refs[:count], refs[-4:-1], refs[-1]
    copies = []
    for i, (to, spot, start) in enumerate(plan):
        place = targets[to].at[spots_ref[spot]]
        width = sources[i].shape[1]
        if width != targets[to].shape[2]:
            place = place.at[:, start : start + width]
        copies.append(pltpu.make_async_copy(sources[i], place, sems.at[i]))
    run_all(copies)


def put_pieces(spots, plan, pieces, targets, shapes):
    anywhere = pl.BlockSpec(memory_space=pl.ANY)
    count = len(pieces)
    return pl.pallas_call(
        functools.partial(put, plan),
        out_shape=tuple(jax.ShapeDtypeStruct(s, pieces[0].dtype) for s in shapes),
        in_specs=[pl.BlockSpec(memory_space=pltpu.SMEM)]
        + [anywhere] * (count + len(targets)),
        out_specs=(anywhere,) * 3,
        scratch_shapes=[pltpu.SemaphoreType.DMA((count,))],
        input_output_aliases={1 + count + i: i for i in range(len(targets))},
        compiler_params=pltpu.CompilerParams(vmem_limit_bytes=2**20),
        name="put_pieces",
    )(spots, *pieces, *targets)


def product(left, right):
    return lax.dot_general(
        left, right, (((1,), (1,)), ((), ())), preferred_element_type=jnp.float32
    )


def quarter_layer(tick_ref, state_ref, pair_ref, *refs):
    up_ref, own_ref, rest_ref, out_ref, hidden_ref, total_ref = refs
    step = up_ref.shape[1]
    block = own_ref.shape[1]
    active = tick_ref[0] == state_ref[0]

    @pl.when(jnp.logical_not(active))
    def _():
        out_ref[...] = jnp.zeros_like(out_ref)

    @pl.when(active)
    def _():
        rows = pair_ref[0].astype(jnp.float32) + pair_ref[1].astype(jnp.float32)
        scale = lax.rsqrt(jnp.mean(rows * rows, axis=1, keepdims=True) + 1e-06)
        normed = (rows * scale).astype(jnp.bfloat16)
        for i in range(SIDE):
            part = jax.nn.gelu(product(normed, up_ref[i])).astype(jnp.bfloat16)
            hidden_ref[:, i * step : (i + 1) * step] = part
        hidden = hidden_ref[...]
        places = [lax.rem(state_ref[2] + offset, SIDE) for offset in OFFSETS]
        for i in range(SIDE):
            total_ref[i, places[0]] = product(hidden, own_ref[i])
            part = product(hidden, rest_ref[i])
            for j in range(SIDE - 1):
                total_ref[i, places[1 + j]] = part[:, j * block : (j + 1) * block]
        pieces = [total_ref[j, i] for i in range(SIDE) for j in range(SIDE)]
        total = jnp.concatenate(pieces, axis=1)
        base = jnp.where(state_ref[1] == 1, rows, 0.0)
        out_ref[...] = (base + total).astype(jnp.bfloat16)


def apply_quarter(tick, state, pair, weights):
    _, row_count, width = pair.shape
    units, block = weights[1].shape[2], weights[1].shape[1]
    resident = pl.BlockSpec(memory_space=pltpu.VMEM)
    scalar = pl.BlockSpec(memory_space=pltpu.SMEM)
    return pl.pallas_call(
        quarter_layer,
        out_shape=jax.ShapeDtypeStruct((row_count, width), jnp.bfloat16),
        in_specs=[scalar] * 2 + [resident] * 4,
        out_specs=resident,
        scratch_shapes=[
            pltpu.VMEM((row_count, units), jnp.bfloat16),
            pltpu.VMEM((SIDE, SIDE, row_count, block), jnp.float32),
        ],
        compiler_params=pltpu.CompilerParams(vmem_limit_bytes=10 * 2**20),
        cost_estimate=pl.CostEstimate(
            flops=4 * row_count * width * units,
            bytes_accessed=4 * row_count * width,
            transcendentals=row_count * units,
        ),
        name="quarter_layer",
    )(tick, state, pair, *weights)


def add_pair(pair_ref, out_ref):
    total = pair_ref[0].astype(jnp.float32) + pair_ref[1].astype(jnp.float32)
    out_ref[...] = total.astype(out_ref.dtype)


def added(pair):
    resident = pl.BlockSpec(memory_space=pltpu.VMEM)
    return pl.pallas_call(
        add_pair,
        out_shape=jax.ShapeDtypeStruct(pair.shape[1:], pair.dtype),
        in_specs=[resident],
        out_specs=resident,
        compiler_params=pltpu.CompilerParams(vmem_limit_bytes=2 * 2**20),
        cost_estimate=pl.CostEstimate(
            flops=pair.size, bytes_accessed=pair.size, transcendentals=0
        ),
        name="add_pair",
    )(pair)


def split_columns(low_ref, block_ref, own_ref, other_ref):
    width = block_ref.shape[1] // SIDE // 2
    low = low_ref[0] == 1
    for i in range(SIDE):
        left = block_ref[:, 2 * i * width : (2 * i + 1) * width]
        right = block_ref[:, (2 * i + 1) * width : (2 * i + 2) * width]
        own_ref[:, i * width : (i + 1) * width] = jnp.where(low, left, right)
        other_ref[:, i * width : (i + 1) * width] = jnp.where(low, right, left)


def own_and_other(low, block):
    rows, width = block.shape
    resident = pl.BlockSpec(memory_space=pltpu.VMEM)
    half = jax.ShapeDtypeStruct((rows, width // 2), block.dtype)
    return pl.pallas_call(
        split_columns,
        out_shape=(half, half),
        in_specs=[pl.BlockSpec(memory_space=pltpu.SMEM), resident],
        out_specs=(resident, resident),
        compiler_params=pltpu.CompilerParams(vmem_limit_bytes=10 * 2**20),
        name="split_columns",
    )(low.reshape(1), block)


def by_halves(low, block, other):
    first = jnp.where(low == 1, block, other)
    second = jnp.where(low == 1, other, block)
    return jnp.concatenate([first, second], axis=0)


def next_plane(layer):
    route = []
    for x, across in INTER:
        for core in range(2):
            to_chip = (x if x < 2 else across) if core == 0 else (x if x >= 2 else across)
            to_core = 0 if x < 2 else 1
            source = (layer * 2 + core) * SIDE + x
            route.append((source, ((layer + 1) * 2 + to_core) * SIDE + to_chip))
    return route


def on_device(layers, patches, w_in, w_out, w_proj):
    plane, core = lax.axis_index("z"), lax.axis_index("c")
    y, x = lax.axis_index("y"), lax.axis_index("x")
    tp = ("y", "x")
    low = (x < 2).astype(jnp.int32)

    own, other = own_and_other(low, w_out[0])
    mate = lax.ppermute(w_in[0], "x", INTRA)
    own_ring, other_ring = ring(own, other, "y")
    beside = lax.ppermute(own, "x", INTRA)
    across = lax.ppermute(other, "x", INTER)
    corner = lax.ppermute(across, "x", INTRA)
    held = (own_ring, other_ring, beside, across)
    own_ring, other_ring, beside, across = lax.optimization_barrier(held)
    own_rest = jnp.concatenate(own_ring, axis=0)
    other_rest = jnp.concatenate(other_ring, axis=0)

    near = by_halves((lax.rem(x, 2) == 0).astype(jnp.int32), w_in[0], mate)
    held = (near, own_rest, other_rest)
    near, own_rest, other_rest = lax.optimization_barrier(held)
    beside_rest = lax.ppermute(own_rest, "x", INTRA)
    across_rest = lax.ppermute(other_rest, "x", INTER)
    corner_rest = lax.ppermute(across_rest, "x", INTRA)
    cut = near.shape[1] // 256 * 128
    below = moved(near, "y", 1)
    above = moved(near, "y", -1)
    head = moved(below[:, :cut], "y", 1)
    tail = moved(above[:, cut:], "y", -1)

    mate_x = x + 1 - 2 * lax.rem(x, 2)
    spots = [lax.rem(y + offset, SIDE) for offset in OFFSETS]
    spots += [x, mate_x, SIDE - 1 - x, SIDE - 1 - mate_x]
    spots = jnp.stack(spots).astype(jnp.int32)
    features, outputs = w_proj.shape
    flat = patches.reshape(-1, features)
    flat = jnp.pad(flat, ((0, 0), (0, outputs - features)))
    everyone = lax.all_gather(jnp.concatenate([flat, w_proj], axis=0), tp, axis=0)
    projection = everyone[:, flat.shape[0] :].reshape(-1, outputs)
    count = flat.shape[0] // SIDE // SIDE

    def rows_of(column):
        at = (SIDE * y + column) * count
        block = lax.dynamic_slice_in_dim(everyone, at, count, axis=1)
        return block[:, :, :features].transpose(1, 0, 2).reshape(count, -1)

    first = jnp.where(low == 1, x, SIDE - 1 - x)
    rows = jnp.concatenate([rows_of(first), rows_of(SIDE - 1 - first)], axis=0)
    adds = jnp.logical_and(core == 0, low == 1)
    state = jnp.stack([plane, adds, y]).astype(jnp.int32)
    pair = jnp.stack([rows, jnp.zeros_like(rows)])
    held = (spots, pair, state, projection)
    spots, pair, state, projection = lax.optimization_barrier(held)
    early = [(near, 0, 0, 0), (below, 0, 1, 0), (above, 0, 2, 0)]
    early += [(own, 1, 4, 0), (beside, 1, 5, 0), (across, 1, 6, 0)]
    early += [(own_rest, 2, 4, 0), (beside_rest, 2, 5, 0), (across_rest, 2, 6, 0)]
    late = [(head, 0, 3, 0), (tail, 0, 3, cut)]
    late += [(corner, 1, 7, 0), (corner_rest, 2, 7, 0)]
    shapes = [(SIDE,) + piece.shape for piece in (near, own, own_rest)]
    weights = ()
    for group in (early, late):
        plan = tuple(entry[1:] for entry in group)
        pieces = [entry[0] for entry in group]
        weights = put_pieces(spots, plan, pieces, weights, shapes)
    weights = [pltpu.with_memory_space_constraint(w, pltpu.VMEM) for w in weights]
    for layer in range(layers):
        tick = jnp.full((1,), layer, jnp.int32)
        part = apply_quarter(tick, state, pair, weights)
        part = added(lax.all_gather(part, "c", axis=0, tiled=False))
        if layer < layers - 1:
            part = lax.ppermute(part, ("z", "c", "x"), next_plane(layer))
            pair = lax.all_gather(part, "c", axis=0, tiled=False)

    count = part.shape[0] // 2
    kept = jnp.where(low == 1, part[:count], part[count:])
    sent = jnp.where(low == 1, part[count:], part[:count])
    last = (layers - 1) * SIDE
    route = [(last + here, last + there) for here, there in INTER]
    got = lax.ppermute(sent, ("z", "x"), route)
    total = kept.astype(jnp.float32) + got.astype(jnp.float32)
    rows = jnp.where(plane == layers - 1, total, 0.0).astype(jnp.bfloat16)
    holders = [layers - 1]
    step = layers // 2
    while step:
        route = [(held, (held + step) % layers) for held in holders]
        rows = rows + lax.ppermute(rows, "z", route)
        holders += [target for _, target in route]
        step //= 2
    return jnp.dot(rows, projection, preferred_element_type=jnp.float32).astype(
        jnp.bfloat16
    )


def solution(mesh):
    sections = mesh.shape["section"]
    grid = Mesh(
        mesh.devices.reshape(sections // 2, 2, SIDE, SIDE), ("z", "c", "y", "x")
    )
    section, tp = ("z", "c"), ("y", "x")
    return jax.shard_map(
        functools.partial(on_device, sections // 2),
        mesh=grid,
        in_specs=(
            P(None, None, tp),
            P(section, tp, None),
            P(section, tp, None),
            P(tp, section),
        ),
        out_specs=P(tp, section),
        check_vma=False,
    )
```

```python
import functools

import jax
import jax.numpy as jnp
from jax import lax
from jax.experimental import pallas as pl
from jax.experimental.pallas import tpu as pltpu
from jax.sharding import Mesh, PartitionSpec as P

SIDE = 4
OFFSETS = (0, 3, 1, 2)
INTRA = [(0, 1), (1, 0), (2, 3), (3, 2)]
INTER = [(0, 3), (3, 0), (1, 2), (2, 1)]


def moved(block, axis, by):
    route = [(i, (i + by) % SIDE) for i in range(SIDE)]
    return lax.ppermute(block, axis, route)


def ring(first, second, axis):
    first_below = moved(first, axis, 1)
    second_above = moved(second, axis, -1)
    second_below = moved(second, axis, 1)
    first_above = moved(first, axis, -1)
    first_far = moved(first_below, axis, 1)
    second_far = moved(second_above, axis, -1)
    return (first_below, first_above, first_far), (second_below, second_above, second_far)


def run_all(copies):
    for copy in copies:
        copy.start()
    for copy in copies:
        copy.wait()


def put(plan, spots_ref, *refs):
    count = len(plan)
    sources, targets, sems = refs[:count], refs[-4:-1], refs[-1]
    copies = []
    for i, (to, spot, start) in enumerate(plan):
        place = targets[to].at[spots_ref[spot]]
        width = sources[i].shape[1]
        if width != targets[to].shape[2]:
            place = place.at[:, start : start + width]
        copies.append(pltpu.make_async_copy(sources[i], place, sems.at[i]))
    run_all(copies)


def put_pieces(spots, plan, pieces, targets, shapes):
    anywhere = pl.BlockSpec(memory_space=pl.ANY)
    count = len(pieces)
    return pl.pallas_call(
        functools.partial(put, plan),
        out_shape=tuple(jax.ShapeDtypeStruct(s, pieces[0].dtype) for s in shapes),
        in_specs=[pl.BlockSpec(memory_space=pltpu.SMEM)]
        + [anywhere] * (count + len(targets)),
        out_specs=(anywhere,) * 3,
        scratch_shapes=[pltpu.SemaphoreType.DMA((count,))],
        input_output_aliases={1 + count + i: i for i in range(len(targets))},
        compiler_params=pltpu.CompilerParams(vmem_limit_bytes=2**20),
        name="put_pieces",
    )(spots, *pieces, *targets)


def product(left, right):
    return lax.dot_general(
        left, right, (((1,), (1,)), ((), ())), preferred_element_type=jnp.float32
    )


def quarter_layer(tick_ref, state_ref, pair_ref, *refs):
    up_ref, own_ref, rest_ref, out_ref, hidden_ref, total_ref = refs
    step = up_ref.shape[1]
    block = own_ref.shape[1]
    active = tick_ref[0] == state_ref[0]

    @pl.when(jnp.logical_not(active))
    def _():
        out_ref[...] = jnp.zeros_like(out_ref)

    @pl.when(active)
    def _():
        rows = pair_ref[0].astype(jnp.float32) + pair_ref[1].astype(jnp.float32)
        scale = lax.rsqrt(jnp.mean(rows * rows, axis=1, keepdims=True) + 1e-06)
        normed = (rows * scale).astype(jnp.bfloat16)
        for i in range(SIDE):
            part = jax.nn.gelu(product(normed, up_ref[i])).astype(jnp.bfloat16)
            hidden_ref[:, i * step : (i + 1) * step] = part
        hidden = hidden_ref[...]
        places = [lax.rem(state_ref[2] + offset, SIDE) for offset in OFFSETS]
        for i in range(SIDE):
            total_ref[i, places[0]] = product(hidden, own_ref[i])
            part = product(hidden, rest_ref[i])
            for j in range(SIDE - 1):
                total_ref[i, places[1 + j]] = part[:, j * block : (j + 1) * block]
        pieces = [total_ref[j, i] for i in range(SIDE) for j in range(SIDE)]
        total = jnp.concatenate(pieces, axis=1)
        base = jnp.where(state_ref[1] == 1, rows, 0.0)
        out_ref[...] = (base + total).astype(jnp.bfloat16)


def apply_quarter(tick, state, pair, weights):
    _, row_count, width = pair.shape
    units, block = weights[1].shape[2], weights[1].shape[1]
    resident = pl.BlockSpec(memory_space=pltpu.VMEM)
    scalar = pl.BlockSpec(memory_space=pltpu.SMEM)
    return pl.pallas_call(
        quarter_layer,
        out_shape=jax.ShapeDtypeStruct((row_count, width), jnp.bfloat16),
        in_specs=[scalar] * 2 + [resident] * 4,
        out_specs=resident,
        scratch_shapes=[
            pltpu.VMEM((row_count, units), jnp.bfloat16),
            pltpu.VMEM((SIDE, SIDE, row_count, block), jnp.float32),
        ],
        compiler_params=pltpu.CompilerParams(vmem_limit_bytes=10 * 2**20),
        cost_estimate=pl.CostEstimate(
            flops=4 * row_count * width * units,
            bytes_accessed=4 * row_count * width,
            transcendentals=row_count * units,
        ),
        name="quarter_layer",
    )(tick, state, pair, *weights)


def add_pair(pair_ref, out_ref):
    total = pair_ref[0].astype(jnp.float32) + pair_ref[1].astype(jnp.float32)
    out_ref[...] = total.astype(out_ref.dtype)


def added(pair):
    resident = pl.BlockSpec(memory_space=pltpu.VMEM)
    return pl.pallas_call(
        add_pair,
        out_shape=jax.ShapeDtypeStruct(pair.shape[1:], pair.dtype),
        in_specs=[resident],
        out_specs=resident,
        compiler_params=pltpu.CompilerParams(vmem_limit_bytes=2 * 2**20),
        cost_estimate=pl.CostEstimate(
            flops=pair.size, bytes_accessed=pair.size, transcendentals=0
        ),
        name="add_pair",
    )(pair)


def split_columns(low_ref, block_ref, own_ref, other_ref):
    width = block_ref.shape[1] // SIDE // 2
    low = low_ref[0] == 1
    for i in range(SIDE):
        left = block_ref[:, 2 * i * width : (2 * i + 1) * width]
        right = block_ref[:, (2 * i + 1) * width : (2 * i + 2) * width]
        own_ref[:, i * width : (i + 1) * width] = jnp.where(low, left, right)
        other_ref[:, i * width : (i + 1) * width] = jnp.where(low, right, left)


def own_and_other(low, block):
    rows, width = block.shape
    resident = pl.BlockSpec(memory_space=pltpu.VMEM)
    half = jax.ShapeDtypeStruct((rows, width // 2), block.dtype)
    return pl.pallas_call(
        split_columns,
        out_shape=(half, half),
        in_specs=[pl.BlockSpec(memory_space=pltpu.SMEM), resident],
        out_specs=(resident, resident),
        compiler_params=pltpu.CompilerParams(vmem_limit_bytes=10 * 2**20),
        name="split_columns",
    )(low.reshape(1), block)


def by_halves(low, block, other):
    first = jnp.where(low == 1, block, other)
    second = jnp.where(low == 1, other, block)
    return jnp.concatenate([first, second], axis=0)


def next_plane(layer):
    route = []
    for x, across in INTER:
        for core in range(2):
            to_chip = (x if x < 2 else across) if core == 0 else (x if x >= 2 else across)
            to_core = 0 if x < 2 else 1
            source = (layer * 2 + core) * SIDE + x
            route.append((source, ((layer + 1) * 2 + to_core) * SIDE + to_chip))
    return route


def on_device(layers, patches, w_in, w_out, w_proj):
    plane, core = lax.axis_index("z"), lax.axis_index("c")
    y, x = lax.axis_index("y"), lax.axis_index("x")
    tp = ("y", "x")
    low = (x < 2).astype(jnp.int32)

    own, other = own_and_other(low, w_out[0])
    own_ring, other_ring = ring(own, other, "y")
    beside = lax.ppermute(own, "x", INTRA)
    across = lax.ppermute(other, "x", INTER)
    corner = lax.ppermute(across, "x", INTRA)
    block, beside = lax.optimization_barrier((w_in[0], beside))
    mate = lax.ppermute(block, "x", INTRA)
    held = (own_ring, other_ring, beside, across)
    own_ring, other_ring, beside, across = lax.optimization_barrier(held)
    own_rest = jnp.concatenate(own_ring, axis=0)
    other_rest = jnp.concatenate(other_ring, axis=0)

    near = by_halves((lax.rem(x, 2) == 0).astype(jnp.int32), block, mate)
    held = (near, own_rest, other_rest)
    near, own_rest, other_rest = lax.optimization_barrier(held)
    near, corner = lax.optimization_barrier((near, corner))
    beside_rest = lax.ppermute(own_rest, "x", INTRA)
    across_rest = lax.ppermute(other_rest, "x", INTER)
    corner_rest = lax.ppermute(across_rest, "x", INTRA)
    cut = near.shape[1] // 256 * 128
    below = moved(near, "y", 1)
    above = moved(near, "y", -1)
    head = moved(below[:, :cut], "y", 1)
    tail = moved(above[:, cut:], "y", -1)

    mate_x = x + 1 - 2 * lax.rem(x, 2)
    spots = [lax.rem(y + offset, SIDE) for offset in OFFSETS]
    spots += [x, mate_x, SIDE - 1 - x, SIDE - 1 - mate_x]
    spots = jnp.stack(spots).astype(jnp.int32)
    features, outputs = w_proj.shape
    flat = patches.reshape(-1, features)
    flat = jnp.pad(flat, ((0, 0), (0, outputs - features)))
    everyone = lax.all_gather(jnp.concatenate([flat, w_proj], axis=0), tp, axis=0)
    projection = everyone[:, flat.shape[0] :].reshape(-1, outputs)
    count = flat.shape[0] // SIDE // SIDE

    def rows_of(column):
        at = (SIDE * y + column) * count
        block = lax.dynamic_slice_in_dim(everyone, at, count, axis=1)
        return block[:, :, :features].transpose(1, 0, 2).reshape(count, -1)

    first = jnp.where(low == 1, x, SIDE - 1 - x)
    rows = jnp.concatenate([rows_of(first), rows_of(SIDE - 1 - first)], axis=0)
    adds = jnp.logical_and(core == 0, low == 1)
    state = jnp.stack([plane, adds, y]).astype(jnp.int32)
    pair = jnp.stack([rows, jnp.zeros_like(rows)])
    held = (spots, pair, state, projection)
    spots, pair, state, projection = lax.optimization_barrier(held)
    early = [(near, 0, 0, 0), (below, 0, 1, 0), (above, 0, 2, 0)]
    early += [(own, 1, 4, 0), (beside, 1, 5, 0), (across, 1, 6, 0)]
    early += [(own_rest, 2, 4, 0), (beside_rest, 2, 5, 0), (across_rest, 2, 6, 0)]
    late = [(head, 0, 3, 0), (tail, 0, 3, cut)]
    late += [(corner, 1, 7, 0), (corner_rest, 2, 7, 0)]
    shapes = [(SIDE,) + piece.shape for piece in (near, own, own_rest)]
    weights = ()
    for group in (early, late):
        plan = tuple(entry[1:] for entry in group)
        pieces = [entry[0] for entry in group]
        weights = put_pieces(spots, plan, pieces, weights, shapes)
    weights = [pltpu.with_memory_space_constraint(w, pltpu.VMEM) for w in weights]
    for layer in range(layers):
        tick = jnp.full((1,), layer, jnp.int32)
        part = apply_quarter(tick, state, pair, weights)
        part = added(lax.all_gather(part, "c", axis=0, tiled=False))
        if layer < layers - 1:
            part = lax.ppermute(part, ("z", "c", "x"), next_plane(layer))
            pair = lax.all_gather(part, "c", axis=0, tiled=False)

    count = part.shape[0] // 2
    kept = jnp.where(low == 1, part[:count], part[count:])
    sent = jnp.where(low == 1, part[count:], part[:count])
    last = (layers - 1) * SIDE
    route = [(last + here, last + there) for here, there in INTER]
    got = lax.ppermute(sent, ("z", "x"), route)
    total = kept.astype(jnp.float32) + got.astype(jnp.float32)
    rows = jnp.where(plane == layers - 1, total, 0.0).astype(jnp.bfloat16)
    holders = [layers - 1]
    step = layers // 2
    while step:
        route = [(held, (held + step) % layers) for held in holders]
        rows = rows + lax.ppermute(rows, "z", route)
        holders += [target for _, target in route]
        step //= 2
    return jnp.dot(rows, projection, preferred_element_type=jnp.float32).astype(
        jnp.bfloat16
    )


def solution(mesh):
    sections = mesh.shape["section"]
    grid = Mesh(
        mesh.devices.reshape(sections // 2, 2, SIDE, SIDE), ("z", "c", "y", "x")
    )
    section, tp = ("z", "c"), ("y", "x")
    return jax.shard_map(
        functools.partial(on_device, sections // 2),
        mesh=grid,
        in_specs=(
            P(None, None, tp),
            P(section, tp, None),
            P(section, tp, None),
            P(tp, section),
        ),
        out_specs=P(tp, section),
        check_vma=False,
    )
```

```python
import functools

import jax
import jax.numpy as jnp
from jax import lax
from jax.experimental import pallas as pl
from jax.experimental.pallas import tpu as pltpu
from jax.sharding import Mesh, PartitionSpec as P

SIDE = 4
OFFSETS = (0, 3, 1, 2)
INTRA = [(0, 1), (1, 0), (2, 3), (3, 2)]
INTER = [(0, 3), (3, 0), (1, 2), (2, 1)]


def moved(block, axis, by):
    route = [(i, (i + by) % SIDE) for i in range(SIDE)]
    return lax.ppermute(block, axis, route)


def ring(first, second, axis):
    first_below = moved(first, axis, 1)
    second_above = moved(second, axis, -1)
    second_below = moved(second, axis, 1)
    first_above = moved(first, axis, -1)
    first_far = moved(first_below, axis, 1)
    second_far = moved(second_above, axis, -1)
    return (first_below, first_above, first_far), (second_below, second_above, second_far)


def run_all(copies):
    for copy in copies:
        copy.start()
    for copy in copies:
        copy.wait()


def put(plan, spots_ref, *refs):
    count = len(plan)
    sources, targets, sems = refs[:count], refs[-4:-1], refs[-1]
    copies = []
    for i, (to, spot, start) in enumerate(plan):
        place = targets[to].at[spots_ref[spot]]
        width = sources[i].shape[1]
        if width != targets[to].shape[2]:
            place = place.at[:, start : start + width]
        copies.append(pltpu.make_async_copy(sources[i], place, sems.at[i]))
    run_all(copies)


def put_pieces(spots, plan, pieces, targets, shapes):
    anywhere = pl.BlockSpec(memory_space=pl.ANY)
    count = len(pieces)
    return pl.pallas_call(
        functools.partial(put, plan),
        out_shape=tuple(jax.ShapeDtypeStruct(s, pieces[0].dtype) for s in shapes),
        in_specs=[pl.BlockSpec(memory_space=pltpu.SMEM)]
        + [anywhere] * (count + len(targets)),
        out_specs=(anywhere,) * 3,
        scratch_shapes=[pltpu.SemaphoreType.DMA((count,))],
        input_output_aliases={1 + count + i: i for i in range(len(targets))},
        compiler_params=pltpu.CompilerParams(vmem_limit_bytes=2**20),
        name="put_pieces",
    )(spots, *pieces, *targets)


def product(left, right):
    return lax.dot_general(
        left, right, (((1,), (1,)), ((), ())), preferred_element_type=jnp.float32
    )


def quarter_layer(tick_ref, state_ref, pair_ref, *refs):
    up_ref, own_ref, rest_ref, out_ref, hidden_ref, total_ref = refs
    step = up_ref.shape[1]
    block = own_ref.shape[1]
    active = tick_ref[0] == state_ref[0]

    @pl.when(jnp.logical_not(active))
    def _():
        out_ref[...] = jnp.zeros_like(out_ref)

    @pl.when(active)
    def _():
        rows = pair_ref[0].astype(jnp.float32) + pair_ref[1].astype(jnp.float32)
        scale = lax.rsqrt(jnp.mean(rows * rows, axis=1, keepdims=True) + 1e-06)
        normed = (rows * scale).astype(jnp.bfloat16)
        for i in range(SIDE):
            part = jax.nn.gelu(product(normed, up_ref[i])).astype(jnp.bfloat16)
            hidden_ref[:, i * step : (i + 1) * step] = part
        hidden = hidden_ref[...]
        places = [lax.rem(state_ref[2] + offset, SIDE) for offset in OFFSETS]
        for i in range(SIDE):
            total_ref[i, places[0]] = product(hidden, own_ref[i])
            part = product(hidden, rest_ref[i])
            for j in range(SIDE - 1):
                total_ref[i, places[1 + j]] = part[:, j * block : (j + 1) * block]
        pieces = [total_ref[j, i] for i in range(SIDE) for j in range(SIDE)]
        total = jnp.concatenate(pieces, axis=1)
        base = jnp.where(state_ref[1] == 1, rows, 0.0)
        out_ref[...] = (base + total).astype(jnp.bfloat16)


def apply_quarter(tick, state, pair, weights):
    _, row_count, width = pair.shape
    units, block = weights[1].shape[2], weights[1].shape[1]
    resident = pl.BlockSpec(memory_space=pltpu.VMEM)
    scalar = pl.BlockSpec(memory_space=pltpu.SMEM)
    return pl.pallas_call(
        quarter_layer,
        out_shape=jax.ShapeDtypeStruct((row_count, width), jnp.bfloat16),
        in_specs=[scalar] * 2 + [resident] * 4,
        out_specs=resident,
        scratch_shapes=[
            pltpu.VMEM((row_count, units), jnp.bfloat16),
            pltpu.VMEM((SIDE, SIDE, row_count, block), jnp.float32),
        ],
        compiler_params=pltpu.CompilerParams(vmem_limit_bytes=10 * 2**20),
        cost_estimate=pl.CostEstimate(
            flops=4 * row_count * width * units,
            bytes_accessed=4 * row_count * width,
            transcendentals=row_count * units,
        ),
        name="quarter_layer",
    )(tick, state, pair, *weights)


def add_pair(pair_ref, out_ref):
    total = pair_ref[0].astype(jnp.float32) + pair_ref[1].astype(jnp.float32)
    out_ref[...] = total.astype(out_ref.dtype)


def added(pair):
    resident = pl.BlockSpec(memory_space=pltpu.VMEM)
    return pl.pallas_call(
        add_pair,
        out_shape=jax.ShapeDtypeStruct(pair.shape[1:], pair.dtype),
        in_specs=[resident],
        out_specs=resident,
        compiler_params=pltpu.CompilerParams(vmem_limit_bytes=2 * 2**20),
        cost_estimate=pl.CostEstimate(
            flops=pair.size, bytes_accessed=pair.size, transcendentals=0
        ),
        name="add_pair",
    )(pair)


def split_columns(low_ref, block_ref, own_ref, other_ref):
    width = block_ref.shape[1] // SIDE // 2
    low = low_ref[0] == 1
    for i in range(SIDE):
        left = block_ref[:, 2 * i * width : (2 * i + 1) * width]
        right = block_ref[:, (2 * i + 1) * width : (2 * i + 2) * width]
        own_ref[:, i * width : (i + 1) * width] = jnp.where(low, left, right)
        other_ref[:, i * width : (i + 1) * width] = jnp.where(low, right, left)


def own_and_other(low, block):
    rows, width = block.shape
    resident = pl.BlockSpec(memory_space=pltpu.VMEM)
    half = jax.ShapeDtypeStruct((rows, width // 2), block.dtype)
    return pl.pallas_call(
        split_columns,
        out_shape=(half, half),
        in_specs=[pl.BlockSpec(memory_space=pltpu.SMEM), resident],
        out_specs=(resident, resident),
        compiler_params=pltpu.CompilerParams(vmem_limit_bytes=10 * 2**20),
        name="split_columns",
    )(low.reshape(1), block)


def by_halves(low, block, other):
    first = jnp.where(low == 1, block, other)
    second = jnp.where(low == 1, other, block)
    return jnp.concatenate([first, second], axis=0)


def next_plane(layer):
    route = []
    for x, across in INTER:
        for core in range(2):
            to_chip = (x if x < 2 else across) if core == 0 else (x if x >= 2 else across)
            to_core = 0 if x < 2 else 1
            source = (layer * 2 + core) * SIDE + x
            route.append((source, ((layer + 1) * 2 + to_core) * SIDE + to_chip))
    return route


def on_device(layers, patches, w_in, w_out, w_proj):
    plane, core = lax.axis_index("z"), lax.axis_index("c")
    y, x = lax.axis_index("y"), lax.axis_index("x")
    tp = ("y", "x")
    low = (x < 2).astype(jnp.int32)

    own, other = own_and_other(low, w_out[0])
    own_ring, other_ring = ring(own, other, "y")
    beside = lax.ppermute(own, "x", INTRA)
    across = lax.ppermute(other, "x", INTER)
    corner = lax.ppermute(across, "x", INTRA)
    block, beside = lax.optimization_barrier((w_in[0], beside))
    mate = lax.ppermute(block, "x", INTRA)
    held = (own_ring, other_ring, beside, across)
    own_ring, other_ring, beside, across = lax.optimization_barrier(held)
    own_rest = jnp.concatenate(own_ring, axis=0)
    other_rest = jnp.concatenate(other_ring, axis=0)

    near = by_halves((lax.rem(x, 2) == 0).astype(jnp.int32), block, mate)
    held = (near, own_rest, other_rest)
    near, own_rest, other_rest = lax.optimization_barrier(held)
    near, corner = lax.optimization_barrier((near, corner))
    beside_rest = lax.ppermute(own_rest, "x", INTRA)
    across_rest = lax.ppermute(other_rest, "x", INTER)
    corner_rest = lax.ppermute(across_rest, "x", INTRA)
    cut = near.shape[1] // 256 * 128
    below = moved(near, "y", 1)
    above = moved(near, "y", -1)
    head = moved(below[:, :cut], "y", 1)
    tail = moved(above[:, cut:], "y", -1)

    mate_x = x + 1 - 2 * lax.rem(x, 2)
    spots = [lax.rem(y + offset, SIDE) for offset in OFFSETS]
    spots += [x, mate_x, SIDE - 1 - x, SIDE - 1 - mate_x]
    spots = jnp.stack(spots).astype(jnp.int32)
    features, outputs = w_proj.shape
    flat = patches.reshape(-1, features)
    flat = jnp.pad(flat, ((0, 0), (0, outputs - features)))
    everyone = lax.all_gather(jnp.concatenate([flat, w_proj], axis=0), tp, axis=0)
    projection = everyone[:, flat.shape[0] :].reshape(-1, outputs)
    count = flat.shape[0] // SIDE // SIDE

    def rows_of(column):
        at = (SIDE * y + column) * count
        block = lax.dynamic_slice_in_dim(everyone, at, count, axis=1)
        return block[:, :, :features].transpose(1, 0, 2).reshape(count, -1)

    first = jnp.where(low == 1, x, SIDE - 1 - x)
    rows = jnp.concatenate([rows_of(first), rows_of(SIDE - 1 - first)], axis=0)
    adds = jnp.logical_and(core == 0, low == 1)
    state = jnp.stack([plane, adds, y]).astype(jnp.int32)
    pair = jnp.stack([rows, jnp.zeros_like(rows)])
    held = (spots, pair, state, projection)
    spots, pair, state, projection = lax.optimization_barrier(held)
    early = [(near, 0, 0, 0), (below, 0, 1, 0), (above, 0, 2, 0)]
    early += [(own, 1, 4, 0), (beside, 1, 5, 0), (across, 1, 6, 0)]
    early += [(own_rest, 2, 4, 0), (beside_rest, 2, 5, 0), (across_rest, 2, 6, 0)]
    late = [(head, 0, 3, 0), (tail, 0, 3, cut)]
    late += [(corner, 1, 7, 0), (corner_rest, 2, 7, 0)]
    shapes = [(SIDE,) + piece.shape for piece in (near, own, own_rest)]
    weights = ()
    for group in (early, late):
        plan = tuple(entry[1:] for entry in group)
        pieces = [entry[0] for entry in group]
        weights = put_pieces(spots, plan, pieces, weights, shapes)
    weights = [pltpu.with_memory_space_constraint(w, pltpu.VMEM) for w in weights]
    for layer in range(layers):
        tick = jnp.full((1,), layer, jnp.int32)
        part = apply_quarter(tick, state, pair, weights)
        part = added(lax.all_gather(part, "c", axis=0, tiled=False))
        if layer < layers - 1:
            part = lax.ppermute(part, ("z", "c", "x"), next_plane(layer))
            pair = lax.all_gather(part, "c", axis=0, tiled=False)

    count = part.shape[0] // 2
    kept = jnp.where(low == 1, part[:count], part[count:])
    sent = jnp.where(low == 1, part[count:], part[:count])
    last, half = layers - 1, layers // 2

    def crossed(target):
        route = [(last * SIDE + i, target * SIDE + j) for i, j in INTER]
        return lax.ppermute(sent, ("z", "x"), route)

    first = (last + half) % layers
    got = crossed(last) + crossed(first)
    ahead = lax.ppermute(kept, "z", [(last, first)])
    kept = jnp.where(plane == last, kept, jnp.zeros_like(kept)) + ahead
    rows = (kept.astype(jnp.float32) + got.astype(jnp.float32)).astype(jnp.bfloat16)
    holders = [last, first]
    step = half // 2
    while step:
        route = [(held, (held + step) % layers) for held in holders]
        rows = rows + lax.ppermute(rows, "z", route)
        holders += [target for _, target in route]
        step //= 2
    return jnp.dot(rows, projection, preferred_element_type=jnp.float32).astype(
        jnp.bfloat16
    )


def solution(mesh):
    sections = mesh.shape["section"]
    grid = Mesh(
        mesh.devices.reshape(sections // 2, 2, SIDE, SIDE), ("z", "c", "y", "x")
    )
    section, tp = ("z", "c"), ("y", "x")
    return jax.shard_map(
        functools.partial(on_device, sections // 2),
        mesh=grid,
        in_specs=(
            P(None, None, tp),
            P(section, tp, None),
            P(section, tp, None),
            P(tp, section),
        ),
        out_specs=P(tp, section),
        check_vma=False,
    )
```

```python
import functools

import jax
import jax.numpy as jnp
from jax import lax
from jax.experimental import pallas as pl
from jax.experimental.pallas import tpu as pltpu
from jax.sharding import Mesh, PartitionSpec as P

SIDE = 4
OFFSETS = (0, 3, 1, 2)
INTRA = [(0, 1), (1, 0), (2, 3), (3, 2)]
INTER = [(0, 3), (3, 0), (1, 2), (2, 1)]


def moved(block, axis, by):
    route = [(i, (i + by) % SIDE) for i in range(SIDE)]
    return lax.ppermute(block, axis, route)


def ring(first, second, axis):
    first_below = moved(first, axis, 1)
    second_above = moved(second, axis, -1)
    second_below = moved(second, axis, 1)
    first_above = moved(first, axis, -1)
    first_far = moved(first_below, axis, 1)
    second_far = moved(second_above, axis, -1)
    return (first_below, first_above, first_far), (second_below, second_above, second_far)


def run_all(copies):
    for copy in copies:
        copy.start()
    for copy in copies:
        copy.wait()


def put(plan, spots_ref, *refs):
    count = len(plan)
    sources, targets, sems = refs[:count], refs[-4:-1], refs[-1]
    copies = []
    for i, (to, spot, start) in enumerate(plan):
        place = targets[to].at[spots_ref[spot]]
        width = sources[i].shape[1]
        if width != targets[to].shape[2]:
            place = place.at[:, start : start + width]
        copies.append(pltpu.make_async_copy(sources[i], place, sems.at[i]))
    run_all(copies)


def put_pieces(spots, plan, pieces, targets, shapes):
    anywhere = pl.BlockSpec(memory_space=pl.ANY)
    count = len(pieces)
    return pl.pallas_call(
        functools.partial(put, plan),
        out_shape=tuple(jax.ShapeDtypeStruct(s, pieces[0].dtype) for s in shapes),
        in_specs=[pl.BlockSpec(memory_space=pltpu.SMEM)]
        + [anywhere] * (count + len(targets)),
        out_specs=(anywhere,) * 3,
        scratch_shapes=[pltpu.SemaphoreType.DMA((count,))],
        input_output_aliases={1 + count + i: i for i in range(len(targets))},
        compiler_params=pltpu.CompilerParams(vmem_limit_bytes=2**20),
        name="put_pieces",
    )(spots, *pieces, *targets)


def product(left, right):
    return lax.dot_general(
        left, right, (((1,), (1,)), ((), ())), preferred_element_type=jnp.float32
    )


def quarter_layer(tick_ref, state_ref, pair_ref, *refs):
    up_ref, own_ref, rest_ref, out_ref, hidden_ref, total_ref = refs
    step = up_ref.shape[1]
    block = own_ref.shape[1]
    active = tick_ref[0] == state_ref[0]

    @pl.when(jnp.logical_not(active))
    def _():
        out_ref[...] = jnp.zeros_like(out_ref)

    @pl.when(active)
    def _():
        rows = pair_ref[0].astype(jnp.float32) + pair_ref[1].astype(jnp.float32)
        scale = lax.rsqrt(jnp.mean(rows * rows, axis=1, keepdims=True) + 1e-06)
        normed = (rows * scale).astype(jnp.bfloat16)
        for i in range(SIDE):
            part = jax.nn.gelu(product(normed, up_ref[i])).astype(jnp.bfloat16)
            hidden_ref[:, i * step : (i + 1) * step] = part
        hidden = hidden_ref[...]
        places = [lax.rem(state_ref[2] + offset, SIDE) for offset in OFFSETS]
        for i in range(SIDE):
            total_ref[i, places[0]] = product(hidden, own_ref[i])
            part = product(hidden, rest_ref[i])
            for j in range(SIDE - 1):
                total_ref[i, places[1 + j]] = part[:, j * block : (j + 1) * block]
        pieces = [total_ref[j, i] for i in range(SIDE) for j in range(SIDE)]
        total = jnp.concatenate(pieces, axis=1)
        base = jnp.where(state_ref[1] == 1, rows, 0.0)
        out_ref[...] = (base + total).astype(jnp.bfloat16)


def apply_quarter(tick, state, pair, weights):
    _, row_count, width = pair.shape
    units, block = weights[1].shape[2], weights[1].shape[1]
    resident = pl.BlockSpec(memory_space=pltpu.VMEM)
    scalar = pl.BlockSpec(memory_space=pltpu.SMEM)
    return pl.pallas_call(
        quarter_layer,
        out_shape=jax.ShapeDtypeStruct((row_count, width), jnp.bfloat16),
        in_specs=[scalar] * 2 + [resident] * 4,
        out_specs=resident,
        scratch_shapes=[
            pltpu.VMEM((row_count, units), jnp.bfloat16),
            pltpu.VMEM((SIDE, SIDE, row_count, block), jnp.float32),
        ],
        compiler_params=pltpu.CompilerParams(vmem_limit_bytes=10 * 2**20),
        cost_estimate=pl.CostEstimate(
            flops=4 * row_count * width * units,
            bytes_accessed=4 * row_count * width,
            transcendentals=row_count * units,
        ),
        name="quarter_layer",
    )(tick, state, pair, *weights)


def add_pair(pair_ref, out_ref):
    total = pair_ref[0].astype(jnp.float32) + pair_ref[1].astype(jnp.float32)
    out_ref[...] = total.astype(out_ref.dtype)


def added(pair):
    resident = pl.BlockSpec(memory_space=pltpu.VMEM)
    return pl.pallas_call(
        add_pair,
        out_shape=jax.ShapeDtypeStruct(pair.shape[1:], pair.dtype),
        in_specs=[resident],
        out_specs=resident,
        compiler_params=pltpu.CompilerParams(vmem_limit_bytes=2 * 2**20),
        cost_estimate=pl.CostEstimate(
            flops=pair.size, bytes_accessed=pair.size, transcendentals=0
        ),
        name="add_pair",
    )(pair)


def split_columns(low_ref, block_ref, own_ref, other_ref):
    width = block_ref.shape[1] // SIDE // 2
    low = low_ref[0] == 1
    for i in range(SIDE):
        left = block_ref[:, 2 * i * width : (2 * i + 1) * width]
        right = block_ref[:, (2 * i + 1) * width : (2 * i + 2) * width]
        own_ref[:, i * width : (i + 1) * width] = jnp.where(low, left, right)
        other_ref[:, i * width : (i + 1) * width] = jnp.where(low, right, left)


def own_and_other(low, block):
    rows, width = block.shape
    resident = pl.BlockSpec(memory_space=pltpu.VMEM)
    half = jax.ShapeDtypeStruct((rows, width // 2), block.dtype)
    return pl.pallas_call(
        split_columns,
        out_shape=(half, half),
        in_specs=[pl.BlockSpec(memory_space=pltpu.SMEM), resident],
        out_specs=(resident, resident),
        compiler_params=pltpu.CompilerParams(vmem_limit_bytes=10 * 2**20),
        name="split_columns",
    )(low.reshape(1), block)


def by_halves(low, block, other):
    first = jnp.where(low == 1, block, other)
    second = jnp.where(low == 1, other, block)
    return jnp.concatenate([first, second], axis=0)


def next_plane(layer):
    route = []
    for x, across in INTER:
        for core in range(2):
            to_chip = (x if x < 2 else across) if core == 0 else (x if x >= 2 else across)
            to_core = 0 if x < 2 else 1
            source = (layer * 2 + core) * SIDE + x
            route.append((source, ((layer + 1) * 2 + to_core) * SIDE + to_chip))
    return route


def on_device(layers, patches, w_in, w_out, w_proj):
    plane, core = lax.axis_index("z"), lax.axis_index("c")
    y, x = lax.axis_index("y"), lax.axis_index("x")
    tp = ("y", "x")
    low = (x < 2).astype(jnp.int32)

    own, other = own_and_other(low, w_out[0])
    own_ring, other_ring = ring(own, other, "y")
    beside = lax.ppermute(own, "x", INTRA)
    across = lax.ppermute(other, "x", INTER)
    corner = lax.ppermute(across, "x", INTRA)
    block, beside = lax.optimization_barrier((w_in[0], beside))
    mate = lax.ppermute(block, "x", INTRA)
    held = (own_ring, other_ring, beside, across)
    own_ring, other_ring, beside, across = lax.optimization_barrier(held)
    own_rest = jnp.concatenate(own_ring, axis=0)
    other_rest = jnp.concatenate(other_ring, axis=0)

    near = by_halves((lax.rem(x, 2) == 0).astype(jnp.int32), block, mate)
    held = (near, own_rest, other_rest)
    near, own_rest, other_rest = lax.optimization_barrier(held)
    near, corner = lax.optimization_barrier((near, corner))
    beside_rest = lax.ppermute(own_rest, "x", INTRA)
    across_rest = lax.ppermute(other_rest, "x", INTER)
    corner_rest = lax.ppermute(across_rest, "x", INTRA)
    cut = near.shape[1] // 256 * 128
    below = moved(near, "y", 1)
    above = moved(near, "y", -1)
    head = moved(below[:, :cut], "y", 1)
    tail = moved(above[:, cut:], "y", -1)

    mate_x = x + 1 - 2 * lax.rem(x, 2)
    spots = [lax.rem(y + offset, SIDE) for offset in OFFSETS]
    spots += [x, mate_x, SIDE - 1 - x, SIDE - 1 - mate_x]
    spots = jnp.stack(spots).astype(jnp.int32)
    features = w_proj.shape[0]
    flat = patches.reshape(-1, features).T
    everyone = lax.all_gather(jnp.concatenate([flat, w_proj], axis=0), tp, axis=0)
    projection = everyone[:, features:].reshape(-1, w_proj.shape[1])
    count = flat.shape[1] // SIDE // SIDE

    def rows_of(column):
        at = (SIDE * y + column) * count
        block = lax.dynamic_slice_in_dim(everyone[:, :features], at, count, axis=2)
        return block.reshape(-1, count).T

    first = jnp.where(low == 1, x, SIDE - 1 - x)
    rows = jnp.concatenate([rows_of(first), rows_of(SIDE - 1 - first)], axis=0)
    adds = jnp.logical_and(core == 0, low == 1)
    state = jnp.stack([plane, adds, y]).astype(jnp.int32)
    pair = jnp.stack([rows, jnp.zeros_like(rows)])
    held = (spots, pair, state, projection)
    spots, pair, state, projection = lax.optimization_barrier(held)
    early = [(near, 0, 0, 0), (below, 0, 1, 0), (above, 0, 2, 0)]
    early += [(own, 1, 4, 0), (beside, 1, 5, 0), (across, 1, 6, 0), (corner, 1, 7, 0)]
    early += [(own_rest, 2, 4, 0), (beside_rest, 2, 5, 0), (across_rest, 2, 6, 0)]
    late = [(head, 0, 3, 0), (tail, 0, 3, cut), (corner_rest, 2, 7, 0)]
    shapes = [(SIDE,) + piece.shape for piece in (near, own, own_rest)]
    weights = ()
    for group in (early, late):
        plan = tuple(entry[1:] for entry in group)
        pieces = [entry[0] for entry in group]
        weights = put_pieces(spots, plan, pieces, weights, shapes)
    weights = [pltpu.with_memory_space_constraint(w, pltpu.VMEM) for w in weights]
    for layer in range(layers):
        tick = jnp.full((1,), layer, jnp.int32)
        part = apply_quarter(tick, state, pair, weights)
        part = added(lax.all_gather(part, "c", axis=0, tiled=False))
        if layer < layers - 1:
            part = lax.ppermute(part, ("z", "c", "x"), next_plane(layer))
            pair = lax.all_gather(part, "c", axis=0, tiled=False)

    count = part.shape[0] // 2
    kept = jnp.where(low == 1, part[:count], part[count:])
    sent = jnp.where(low == 1, part[count:], part[:count])
    last, half = layers - 1, layers // 2

    def crossed(target):
        route = [(last * SIDE + i, target * SIDE + j) for i, j in INTER]
        return lax.ppermute(sent, ("z", "x"), route)

    first = (last + half) % layers
    got = crossed(last) + crossed(first)
    ahead = lax.ppermute(kept, "z", [(last, first)])
    kept = jnp.where(plane == last, kept, jnp.zeros_like(kept)) + ahead
    rows = (kept.astype(jnp.float32) + got.astype(jnp.float32)).astype(jnp.bfloat16)
    holders = [last, first]
    step = half // 2
    while step:
        route = [(held, (held + step) % layers) for held in holders]
        rows = rows + lax.ppermute(rows, "z", route)
        holders += [target for _, target in route]
        step //= 2
    return jnp.dot(rows, projection, preferred_element_type=jnp.float32).astype(
        jnp.bfloat16
    )


def solution(mesh):
    sections = mesh.shape["section"]
    grid = Mesh(
        mesh.devices.reshape(sections // 2, 2, SIDE, SIDE), ("z", "c", "y", "x")
    )
    section, tp = ("z", "c"), ("y", "x")
    return jax.shard_map(
        functools.partial(on_device, sections // 2),
        mesh=grid,
        in_specs=(
            P(None, None, tp),
            P(section, tp, None),
            P(section, tp, None),
            P(tp, section),
        ),
        out_specs=P(tp, section),
        check_vma=False,
    )
```
